128 devices in a mesh: dp: 32 (over z, y, x_hi), mp: 2 (over x_lo), grid: 2 (over core).
Axes of the slice: x: 4 (x_hi: 2, x_lo: 2; x = x_hi * 2 + x_lo), y: 4, z: 4, core: 2. Of those that a mesh axis runs over, the one named last changes fastest.
Arguments:
- tokens: bfloat16 [16384, 768], P(('dp', 'grid')), may hold values from -6 to 6
- seq_lengths: int32 [32], P('dp'), may hold values from 257 to 512, as said below
- cotangent: bfloat16 [16384, 768], P(('dp', 'grid')), may hold values from -6 to 6
- qkv_weight: bfloat16 [3, 768, 768], P(None, 'mp'), may hold values from -0.21875 to 0.21875
- qv_bias: float32 [2, 768], P(None, 'mp'), may hold values from -1.2 to 1.2
- out_weight: bfloat16 [768, 768], P('mp'), may hold values from -0.875 to 0.875
- out_bias: float32 [768], replicated, may hold values from -2 to 2
- first_gain: float32 [768], replicated, may hold values from 0.5 to 1.5
- first_shift: float32 [768], replicated, may hold values from -2 to 2
- second_gain: float32 [768], replicated, may hold values from 0.5 to 1.5
- second_shift: float32 [768], replicated, may hold values from -2 to 2
- up_weight: bfloat16 [768, 3072], P('mp', 'grid'), may hold values from -0.21875 to 0.21875
- up_bias: float32 [3072], P('grid'), may hold values from -3 to 3
- down_weight: bfloat16 [768, 3072], P('mp', 'grid'), may hold values from -0.21875 to 0.21875
- down_bias: float32 [768], P('mp'), may hold values from -2 to 2
Outputs:
- layer_out: bfloat16 [16384, 768], P(('dp', 'grid'), 'mp')
- input_grad: float32 [16384, 768], P(('dp', 'grid'))
- grad_qkv_weight: float32 [3, 768, 768], P(None, 'mp')
- grad_qv_bias: float32 [2, 768], P(None, 'mp')
- grad_out_weight: float32 [768, 768], P('mp')
- grad_out_bias: float32 [768], replicated
- grad_first_gain: float32 [768], replicated
- grad_first_shift: float32 [768], replicated
- grad_second_gain: float32 [768], replicated
- grad_second_shift: float32 [768], replicated
- grad_up_weight: float32 [768, 3072], P('mp', 'grid')
- grad_up_bias: float32 [3072], P('grid')
- grad_down_weight: float32 [768, 3072], P('mp', 'grid')
- grad_down_bias: float32 [768], P('mp')
The draws below stay inside these ranges and needn't reach their ends.
Inputs may be any that keep to these rules, and one draw needn't show every extreme that they name: Group g holds one sequence in its first seq_lengths[g] rows; every later row of the group is a padding row that sees only itself. Some group is full in every draw.
All inputs are finite; a program needn't handle non-finite values.
Results may differ from the reference program's by a relative error of at most 0.0085.
Values may be sent and summed in bfloat16 or wider, within the bound.
A program may use at most 128 MiB of HBM per device.

```python
import jax
import jax.numpy as jnp
from jax import lax

D = 768
HD = 64
FF = 3072
RPD = 256
ROWS_GRP = 512
TOKENS = 16384
N_DP = 32
N_GRID = 2


def draw_seq_lengths(key, part):
    group_rows = RPD * N_GRID
    first_key, second_key = jax.random.split(jax.random.fold_in(key, 7))
    drawn_rows = jax.random.randint(first_key, (N_DP,), group_rows - RPD + 1, group_rows + 1)
    chosen = jax.random.randint(second_key, (), 0, N_DP)
    return jnp.where(jnp.arange(N_DP) == chosen, group_rows, drawn_rows).astype(jnp.int32)


def block_levels(key, shape, pieces, low, largest):
    level, own = 1.0, jax.random.fold_in(key, 6)
    for dim, parts in pieces:
        heights = jnp.exp(jax.random.uniform(jax.random.fold_in(own, dim), (parts,), jnp.float32, low / len(pieces), largest / len(pieces)))
        level = level * jnp.repeat(heights, shape[dim] // parts).reshape([-1 if axis == dim else 1 for axis in range(len(shape))])
    return level


def noise(own_key, extent, width, most, shards=(), kind=jnp.bfloat16):
    values = jax.random.normal(own_key, extent, jnp.float32) * width
    if len(shards) > 0:
        values = block_levels(own_key, extent, shards, -0.22, 0.18) * values
    return jnp.clip(values, min=-most, max=most).astype(kind)


def setup_inputs(seed: int = 0) -> dict:
    seeds = jax.random.split(jax.random.key(seed), 16)
    return {
        "tokens": noise(seeds[0], (TOKENS, D), 1.0, 6.0, ((0, 64),)),
        "seq_lengths": draw_seq_lengths(jax.random.fold_in(seeds[15], 71), 0),
        "cotangent": noise(seeds[2], (TOKENS, D), 1.0, 6.0, ((0, 64),)),
        "qkv_weight": noise(seeds[3], (3, D, D), D ** -0.5, 0.21875, ((1, 2),)),
        "qv_bias": noise(seeds[4], (2, D), 0.2, 1.2, ((1, 2),), jnp.float32),
        "out_weight": noise(seeds[5], (D, D), (max(D // 16, 1)) ** -0.5, 0.875, ((0, 2),)),
        "out_bias": noise(seeds[6], (D,), 0.3, 2.0, (), jnp.float32),
        "first_gain": jnp.clip(1.0 + 0.1 * jax.random.normal(seeds[7], (D,), jnp.float32), 0.5, 1.5),
        "first_shift": noise(seeds[8], (D,), 0.3, 2.0, (), jnp.float32),
        "second_gain": jnp.clip(1.0 + 0.1 * jax.random.normal(seeds[9], (D,), jnp.float32), 0.5, 1.5),
        "second_shift": noise(seeds[10], (D,), 0.3, 2.0, (), jnp.float32),
        "up_weight": noise(seeds[11], (D, FF), D ** -0.5, 0.21875, ((0, 2), (1, 2))),
        "up_bias": noise(seeds[12], (FF,), 0.5, 3.0, ((0, 2),), jnp.float32),
        "down_weight": noise(seeds[13], (D, FF), (FF // 4) ** -0.5, 0.21875, ((0, 2), (1, 2))),
        "down_bias": noise(seeds[14], (D,), 0.3, 2.0, ((0, 2),), jnp.float32),
    }


EPS = 1e-05
NEG = -1e+30

@jax.custom_vjp
def low(v):
    return lax.optimization_barrier(v.astype(jnp.bfloat16)).astype(jnp.float32)

@jax.custom_vjp
def low_back(v):
    return v

def low_keep(v):
    return (low(v), None)

def low_pass(kept, grad):
    return (grad,)

def back_keep(v):
    return (v, None)

def back_low(kept, grad):
    return (low(grad),)
low.defvjp(low_keep, low_pass)
low_back.defvjp(back_keep, back_low)

def matmul_hi(left, right):
    return jnp.dot(left, right, precision=lax.Precision.HIGHEST)

def matmul_hi_t(left, right):
    return lax.dot_general(left, right, (((1,), (1,)), ((), ())), precision=lax.Precision.HIGHEST)

def layer_norm(values, gain, shift):
    mean_row = lax.optimization_barrier(jnp.mean(values, axis=-1, keepdims=True))
    centred = values - mean_row
    spread = lax.optimization_barrier(jnp.mean(centred * centred, axis=-1, keepdims=True))
    return centred * lax.rsqrt(spread + EPS) * gain + shift

def visible(query_pos, key_pos, length):
    same_row = key_pos[None, :] == query_pos[:, None]
    earlier = (key_pos[None, :] < query_pos[:, None]) & (query_pos[:, None] < length)
    return same_row | earlier

def group_forward(rows_in, length, qkv_weight, qv_bias, out_weight, out_bias, first_gain, first_shift, second_gain, second_shift, up_weight, up_bias, down_weight, down_bias):
    row_count = rows_in.shape[0]
    head_count = D // HD
    score_scale = HD ** (-0.5)
    normed1 = low(layer_norm(rows_in, first_gain, first_shift))
    queries = low(low_back(matmul_hi_t(normed1, qkv_weight[0]) + qv_bias[0]))
    keys_all = low(low_back(matmul_hi_t(normed1, qkv_weight[1])))
    values_all = low(low_back(matmul_hi_t(normed1, qkv_weight[2]) + qv_bias[1]))
    key_heads = keys_all.reshape(row_count, head_count, HD)
    value_heads = values_all.reshape(row_count, head_count, HD)
    block_rows = min(512, row_count)
    key_pos = jnp.arange(row_count, dtype=jnp.int32)

    def attend(item):
        query_block, first_row = item
        query_heads = query_block.reshape(block_rows, head_count, HD)
        query_pos = first_row + jnp.arange(block_rows, dtype=jnp.int32)
        scores = jnp.einsum('qhd,khd->hqk', query_heads, key_heads, precision=lax.Precision.HIGHEST) * score_scale
        scores = low_back(scores)
        allowed = visible(query_pos, key_pos, length)[None]
        scores = jnp.where(allowed, scores, NEG)
        row_max = lax.optimization_barrier(jnp.max(scores, axis=-1, keepdims=True))
        expd = jnp.where(allowed, jnp.exp(scores - row_max), 0.0)
        probs_low = low(expd / lax.optimization_barrier(jnp.sum(expd, axis=-1, keepdims=True)))
        mixed = jnp.einsum('hqk,khd->qhd', probs_low, value_heads, precision=lax.Precision.HIGHEST)
        return mixed.reshape(block_rows, D)
    starts = jnp.arange(row_count // block_rows, dtype=jnp.int32) * block_rows
    attended = lax.map(jax.checkpoint(attend), (queries.reshape(row_count // block_rows, block_rows, D), starts))
    attended = low(low_back(attended.reshape(row_count, D)))
    branch = low_back(matmul_hi(attended, out_weight) + out_bias)
    hidden1 = rows_in + branch
    normed2 = low(layer_norm(hidden1, second_gain, second_shift))
    pre_act = low_back(matmul_hi(normed2, up_weight) + up_bias)
    hidden = low(jax.nn.gelu(pre_act, approximate=True))
    return hidden1 + matmul_hi_t(hidden, down_weight) + down_bias

def reference(tokens, seq_lengths, cotangent, qkv_weight, qv_bias, out_weight, out_bias, first_gain, first_shift, second_gain, second_shift, up_weight, up_bias, down_weight, down_bias):
    params = tuple((p.astype(jnp.float32) for p in (qkv_weight, qv_bias, out_weight, out_bias, first_gain, first_shift, second_gain, second_shift, up_weight, up_bias, down_weight, down_bias)))

    def run(rows_all, *weights):
        groups = rows_all.reshape(N_DP, ROWS_GRP, D)
        outputs = lax.map(lambda item: group_forward(item[0], item[1], *weights), (groups, seq_lengths))
        return outputs.reshape(N_DP * ROWS_GRP, D)
    result, pullback = jax.vjp(run, tokens.astype(jnp.float32), *params)
    grads = pullback(cotangent.astype(jnp.float32))
    return (result.astype(jnp.bfloat16), grads[0], grads[1], grads[2], grads[3], grads[4], grads[5], grads[6], grads[7], grads[8], grads[9], grads[10], grads[11], grads[12])
```

```python
import functools

import jax
import jax.numpy as jnp
from jax import lax
from jax.experimental import pallas as pl
from jax.experimental.pallas import tpu as pltpu
from jax.sharding import PartitionSpec as P

HD = 64
EPS = 1e-05
NEG = -1e30
MESH = pl.DeviceIdType.MESH
F32, BF16 = jnp.float32, jnp.bfloat16
def place():
    dp = lax.axis_index("dp")
    xh = lax.rem(dp, 2); y = lax.rem(lax.div(dp, 2), 4); z = lax.div(dp, 8)
    def at(z, y, xh):
        return {"dp": z * 8 + y * 2 + xh}
    y1 = y + 1 - 2 * lax.rem(y, 2)
    z1 = z + 1 - 2 * lax.rem(z, 2)
    peers = [at(z, y1, xh), at(z1, y, xh), at(z, 3 - y, xh), at(3 - z, y, xh), at(z, y, 1 - xh)]
    bits = [lax.rem(lax.div(y + 1, 2), 2), lax.rem(lax.div(z + 1, 2), 2), lax.div(y, 2), lax.div(z, 2), xh]
    return peers, bits

def ar_kernel(R, g_ref, out_ref, acc, sbuf, rbuf, ssem, rsem, asem, bsem):
    Q = R // 4
    peers, bits = place()
    bar = pltpu.get_barrier_semaphore()
    for p in peers:
        pl.semaphore_signal(bar, inc=1, device_id=p, device_id_type=MESH)
    pl.semaphore_wait(bar, 5)
    C = R // 64
    def rs_copy(s, k):
        L = Q >> (min(k, 3) + 1)
        o = s * Q + (Q - (Q >> k))
        d = (s + k) % 4 if k < 4 else 4
        return pltpu.make_async_remote_copy(
            src_ref=sbuf.at[pl.ds(o, L)], dst_ref=rbuf.at[pl.ds(o, L)],
            send_sem=ssem.at[s, k], recv_sem=rsem.at[s, k], device_id=peers[d], device_id_type=MESH)
    offs = [jnp.int32(s * Q) for s in range(4)]
    m8 = lambda v: pl.multiple_of(v, 16)
    hist = []
    for k in range(4):
        L = Q >> (k + 1)
        keep, give = [], []
        for s in range(4):
            b = bits[(s + k) % 4]
            keep.append(offs[s] + b * L); give.append(offs[s] + (1 - b) * L)
        for s in range(4):
            if k > 0:
                rs_copy(s, k - 1).wait_recv()
            so = s * Q + (Q - (Q >> k))
            po = s * Q + (Q - (Q >> (k - 1))) if k > 0 else 0
            go = give[s]
            rel = go - offs[s]
            @pl.loop(0, L // C)
            def _(i):
                v = (g_ref if k < 2 else acc)[pl.ds(m8(go + i * C), C), :]
                if k > 0:
                    v = v + rbuf[pl.ds(m8(po + rel + i * C), C), :].astype(F32)
                sbuf[pl.ds(m8(so + i * C), C), :] = v.astype(BF16)
            rs_copy(s, k).start()
        if k > 0:
            for s in range(4):
                ko = keep[s]
                rel = ko - offs[s]
                po = s * Q + (Q - (Q >> (k - 1)))
                @pl.loop(0, L // C)
                def _(i):
                    acc[pl.ds(m8(ko + i * C), C), :] = (g_ref if k == 1 else acc)[pl.ds(m8(ko + i * C), C), :] + rbuf[pl.ds(m8(po + rel + i * C), C), :].astype(F32)
        hist.append(list(offs))
        offs = keep
    xh = bits[4]
    L = Q // 16
    for s in range(4):
        rs_copy(s, 3).wait_recv()
    for j in range(2):
        for s in (2 * j, 2 * j + 1):
            po = s * Q + (Q - (Q >> 3))
            so = s * Q + (Q - (Q >> 4))
            sbuf[pl.ds(so, L), :] = (acc[pl.ds(m8(offs[s]), L), :] + rbuf[pl.ds(po, L), :].astype(F32)).astype(BF16)
    def x_copy(j):
        o = (2 * j + (1 - xh)) * Q + Q - (Q >> 4)
        return pltpu.make_async_remote_copy(
            src_ref=sbuf.at[pl.ds(m8(o), L)], dst_ref=rbuf.at[pl.ds(m8(o), L)],
            send_sem=ssem.at[j, 4], recv_sem=rsem.at[j, 4], device_id=peers[4], device_id_type=MESH)
    for j in range(2):
        x_copy(j).start()
    for j in range(2):
        x_copy(j).wait_recv()
    def fin_off(j, h):
        return jnp.where(h == 0, offs[2 * j], offs[2 * j + 1]) if False else offs[2 * j] + h * (offs[2 * j + 1] - offs[2 * j])
    def ax_copy(j):
        o = fin_off(j, xh)
        return pltpu.make_async_remote_copy(
            src_ref=out_ref.at[pl.ds(m8(o), L)], dst_ref=out_ref.at[pl.ds(m8(o), L)],
            send_sem=asem.at[j, 4], recv_sem=bsem.at[j, 4], device_id=peers[4], device_id_type=MESH)
    for j in range(2):
        s = 2 * j + xh
        po = m8(s * Q + (Q - (Q >> 3)))
        ro = m8(s * Q + (Q - (Q >> 4)))
        fo = m8(fin_off(j, xh))
        out_ref[pl.ds(fo, L), :] = (acc[pl.ds(fo, L), :] + rbuf[pl.ds(po, L), :].astype(F32) + rbuf[pl.ds(ro, L), :].astype(F32)).astype(BF16)
        ax_copy(j).start()
    for j in range(2):
        ax_copy(j).wait_recv()
    def ag_copy(s, k):
        L = Q >> (k + 1)
        d = (s + k) % 4
        o = m8(hist[k][s] + bits[d] * L)
        return pltpu.make_async_remote_copy(
            src_ref=out_ref.at[pl.ds(o, L)], dst_ref=out_ref.at[pl.ds(o, L)],
            send_sem=asem.at[s, k], recv_sem=bsem.at[s, k], device_id=peers[d], device_id_type=MESH)
    for k in (3, 2, 1, 0):
        for s in range(4):
            if k < 3:
                ag_copy(s, k + 1).wait_recv()
            ag_copy(s, k).start()
    for s in range(4):
        ag_copy(s, 0).wait_recv()
    for s in range(4):
        for k in range(4):
            rs_copy(s, k).wait_send()
            ag_copy(s, k).wait_send()
    for j in range(2):
        x_copy(j).wait_send()
        ax_copy(j).wait_send()

def all_reduce(g, cid):
    R = g.shape[0]
    return pl.pallas_call(
        functools.partial(ar_kernel, R),
        out_shape=jax.ShapeDtypeStruct((R, 128), BF16),
        in_specs=[pl.BlockSpec(memory_space=pltpu.VMEM)],
        out_specs=pl.BlockSpec(memory_space=pltpu.VMEM),
        scratch_shapes=[pltpu.VMEM((R, 128), F32), pltpu.VMEM((R, 128), BF16), pltpu.VMEM((R, 128), BF16)] + [pltpu.SemaphoreType.DMA((4, 5))] * 4,
        compiler_params=pltpu.CompilerParams(collective_id=cid, has_side_effects=True, vmem_limit_bytes=40 << 20),
        name="ar",
    )(g)


def dot(left, right, left_dim, right_dim):
    return lax.dot_general(
        left, right, (((left_dim,), (right_dim,)), ((), ())), preferred_element_type=F32
    )


def norm_stats(values):
    mean_row = jnp.mean(values, axis=-1, keepdims=True)
    centred = values - mean_row
    spread = jnp.mean(centred * centred, axis=-1, keepdims=True)
    scale = lax.rsqrt(spread + EPS)
    return centred * scale, scale


def gelu_parts(pre):
    c = 0.7978845608028654
    inner = c * (pre + 0.044715 * pre * pre * pre)
    t = jnp.tanh(inner)
    hidden = 0.5 * pre * (1.0 + t)
    slope = 0.5 * (1.0 + t) + 0.5 * pre * (1.0 - t * t) * (c * (1.0 + 3 * 0.044715 * pre * pre))
    return hidden, slope


def stage_attend(x, length, qkv, qv_bias, gain, shift):
    n1, _ = norm_stats(x.astype(F32))
    normed1 = (n1 * gain + shift).astype(BF16)
    q = (dot(normed1, qkv[0], 1, 1) + qv_bias[0]).astype(BF16)
    k = dot(normed1, qkv[1], 1, 1).astype(BF16)
    v = (dot(normed1, qkv[2], 1, 1) + qv_bias[1]).astype(BF16)
    probs_all, att = [], []
    rows = x.shape[0]
    qp = lax.broadcasted_iota(jnp.int32, (rows, rows), 0)
    kp = lax.broadcasted_iota(jnp.int32, (rows, rows), 1)
    allowed = (kp == qp) | ((kp < qp) & (qp < length))
    for h in range(q.shape[1] // HD):
        sl = slice(h * HD, (h + 1) * HD)
        s = jnp.where(allowed, dot(q[:, sl], k[:, sl], 1, 1) * HD**-0.5, NEG)
        e = jnp.where(allowed, jnp.exp(s - jnp.max(s, axis=-1, keepdims=True)), 0.0)
        p = e / jnp.sum(e, axis=-1, keepdims=True)
        probs_all.append(p)
        att.append(dot(p.astype(BF16), v[:, sl], 1, 0))
    return normed1, q, k, v, probs_all, jnp.concatenate(att, axis=1).astype(BF16)


def per_device(tokens, seq_lengths, cotangent, qkv_weight, qv_bias, out_weight, out_bias,
               first_gain, first_shift, second_gain, second_shift, up_weight, up_bias, down_weight, down_bias):
    j, i = lax.axis_index("grid"), lax.axis_index("mp")
    rpd = tokens.shape[0]
    own = qkv_weight.shape[1] // 2
    part = out_weight.shape[0]
    up_all = lax.all_gather(up_weight, "mp", axis=0, tiled=True)
    down_all = lax.all_gather(down_weight, "mp", axis=0, tiled=True)
    out_all = lax.all_gather(out_weight, "mp", axis=0, tiled=True)
    x = lax.all_gather(tokens, "grid", axis=0, tiled=True)
    cot = lax.all_gather(cotangent, "grid", axis=0, tiled=True)
    qkv = lax.dynamic_slice_in_dim(qkv_weight, own * j, own, 1)
    qvb = lax.dynamic_slice_in_dim(qv_bias, own * j, own, 1)
    out_own = lax.dynamic_slice_in_dim(out_weight, own * j, own, 0)
    normed1, q, k, v, probs, att = stage_attend(x, seq_lengths[0], qkv, qvb, first_gain, first_shift)
    att_all = lax.all_gather(att, ("mp", "grid"), axis=1, tiled=True)
    hidden1 = x.astype(F32) + dot(att_all, out_all, 1, 0) + out_bias
    n2, scale2 = norm_stats(hidden1)
    normed2 = (n2 * second_gain + second_shift).astype(BF16)
    pre = dot(normed2, up_all, 1, 0) + up_bias
    hidden, slope = gelu_parts(pre)
    hidden = hidden.astype(BF16)
    cot_part = lax.dynamic_slice_in_dim(cot, part * i, part, 1)
    n2_part = lax.dynamic_slice_in_dim(normed2, part * i, part, 1)
    mlp = lax.psum_scatter(dot(hidden, down_weight, 1, 1), "grid", scatter_dimension=0, tiled=True)
    h1_part = lax.dynamic_slice(hidden1, (rpd * j, part * i), (rpd, part))
    layer_out = (h1_part + mlp + down_bias).astype(BF16)
    grad_down = dot(cot_part, hidden, 0, 0)
    grad_down_bias = jnp.sum(cot_part.astype(F32), axis=0)
    grad_pre = (dot(cot, down_all, 1, 0) * slope).astype(BF16)
    grad_up = dot(n2_part, grad_pre, 0, 0)
    grad_up_bias = jnp.sum(grad_pre.astype(F32), axis=0)
    gn2 = lax.psum(dot(grad_pre, up_all, 1, 1), "grid")
    cotf = cot.astype(F32)
    e2 = gn2 * second_gain
    gh1 = cotf + (e2 - jnp.mean(e2, -1, keepdims=True) - n2 * jnp.mean(e2 * n2, -1, keepdims=True)) * scale2
    g2gain = jnp.sum(gn2 * n2, axis=0)
    g2shift = jnp.sum(gn2, axis=0)
    gb = gh1.astype(BF16)
    grad_out = dot(att, gb, 0, 0)
    grad_out_bias = jnp.sum(gb.astype(F32), axis=0)
    gatt = dot(gb, out_own, 1, 1).astype(BF16)
    gq, gk, gv = [], [], []
    for h in range(own // HD):
        sl = slice(h * HD, (h + 1) * HD)
        gp = dot(gatt[:, sl], v[:, sl], 1, 1)
        delta = jnp.sum(probs[h] * gp, axis=-1, keepdims=True)
        gs = (probs[h] * (gp - delta)).astype(BF16)
        gq.append(dot(gs, k[:, sl], 1, 0) * HD**-0.5)
        gk.append(dot(gs, q[:, sl], 0, 0) * HD**-0.5)
        gv.append(dot(probs[h].astype(BF16), gatt[:, sl], 0, 0))
    g3 = [jnp.concatenate(g, axis=1).astype(BF16) for g in (gq, gk, gv)]
    grad_qkv = jnp.concatenate([dot(g, normed1, 0, 0) for g in g3], axis=0)
    gqvb = jnp.stack([jnp.sum(g3[0].astype(F32), 0), jnp.sum(g3[2].astype(F32), 0)])
    gn1 = dot(g3[0], qkv[0], 1, 0) + dot(g3[1], qkv[1], 1, 0) + dot(g3[2], qkv[2], 1, 0)
    n1, scale1 = norm_stats(x.astype(F32))
    g1 = lax.psum(jnp.stack([jnp.sum(gn1 * n1, 0), jnp.sum(gn1, 0)]), ("mp", "grid"))
    gn1_mine = lax.psum(lax.psum_scatter(gn1, "grid", scatter_dimension=0, tiled=True), "mp")
    mine = lambda a: lax.dynamic_slice_in_dim(a, rpd * j, rpd, 0)
    e1 = gn1_mine * first_gain
    n1m = mine(n1)
    input_grad = mine(gh1) + (
        e1 - jnp.mean(e1, -1, keepdims=True) - n1m * jnp.mean(e1 * n1m, -1, keepdims=True)
    ) * mine(scale1)
    mlp_flat = jnp.concatenate([grad_up.reshape(-1, 128), grad_down.reshape(-1, 128)])
    smalls = [gqvb, grad_out_bias, g1, g2gain, g2shift, grad_up_bias, grad_down_bias]
    flat = jnp.concatenate([a.reshape(-1) for a in smalls])
    attn_flat = jnp.concatenate([grad_qkv.reshape(-1, 128), grad_out.reshape(-1, 128)])
    rows = 1024 - attn_flat.shape[0] % 1024
    attn_flat = jnp.concatenate([attn_flat, jnp.pad(flat, (0, rows * 128 - flat.shape[0])).reshape(rows, 128)])
    red = all_reduce(jnp.concatenate([mlp_flat, attn_flat]), 0).astype(F32)
    n_mlp = mlp_flat.shape[0]
    r_up = red[: n_mlp // 2].reshape(grad_up.shape)
    r_down = red[n_mlp // 2 : n_mlp].reshape(grad_down.shape)
    r_qkv = red[n_mlp : n_mlp + 3 * own * 6].reshape(3, own, 768)
    r_out = red[n_mlp + 18 * own : n_mlp + 24 * own].reshape(own, 768)
    sm = red[n_mlp + 24 * own :].reshape(-1)
    res, at = [], 0
    for a in smalls:
        res.append(sm[at : at + a.size].reshape(a.shape))
        at += a.size
    r_qkv = lax.all_gather(r_qkv.astype(BF16), "grid", axis=1, tiled=True).astype(F32)
    r_out = lax.all_gather(r_out.astype(BF16), "grid", axis=0, tiled=True).astype(F32)
    r_qvb = lax.all_gather(res[0], "grid", axis=1, tiled=True)
    return (layer_out, input_grad, r_qkv, r_qvb, r_out, res[1], res[2][0], res[2][1], res[3], res[4],
            r_up, res[5], r_down, res[6])


def solution(mesh):
    placed = (
        P(("dp", "grid"), None), P("dp"), P(("dp", "grid"), None), P(None, "mp", None), P(None, "mp"),
        P("mp", None), P(), P(), P(), P(), P(), P("mp", "grid"), P("grid"), P("mp", "grid"), P("mp"),
    )
    return jax.shard_map(
        per_device,
        mesh=mesh,
        in_specs=placed,
        out_specs=(
            P(("dp", "grid"), "mp"), P(("dp", "grid"), None), P(None, "mp", None), P(None, "mp"), P("mp", None),
            P(), P(), P(), P(), P(), P("mp", "grid"), P("grid"), P("mp", "grid"), P("mp"),
        ),
        check_vma=False,
    )
```

```python
import functools

import jax
import jax.numpy as jnp
from jax import lax
from jax.experimental import pallas as pl
from jax.experimental.pallas import tpu as pltpu
from jax.sharding import PartitionSpec as P

HD = 64
EPS = 1e-05
NEG = -1e30
MESH = pl.DeviceIdType.MESH
F32, BF16 = jnp.float32, jnp.bfloat16


def dot(left, right, left_dim, right_dim):
    return lax.dot_general(
        left, right, (((left_dim,), (right_dim,)), ((), ())), preferred_element_type=F32
    )


def up16(value):
    return pl.multiple_of(value, 16)


def cols128(start, size):
    return pl.ds(pl.multiple_of(start, 128), size)


class Place:
    def __init__(self):
        dp = lax.axis_index("dp")
        self.i, self.j = lax.axis_index("mp"), lax.axis_index("grid")
        self.xh, self.y, self.z = lax.rem(dp, 2), lax.rem(lax.div(dp, 2), 4), lax.div(dp, 8)
        self.sib = {"grid": 1 - self.j}
        self.xa = {"mp": 1 - self.i}
        self.xb = {"dp": dp + 1 - 2 * self.xh, "mp": 1 - self.i}
        self.xc = {"mp": 1 - self.i, "grid": 1 - self.j}
        self.far = {"dp": dp + 1 - 2 * self.xh}
        self.ring = (
            [{"dp": dp + 2 * (lax.rem(self.y + d, 4) - self.y)} for d in (1, 2, 3)],
            [{"dp": dp + 8 * (lax.rem(self.z + d, 4) - self.z)} for d in (1, 2, 3)],
        )

    def all(self):
        return [self.sib, self.xa, self.xb, self.xc, self.far] + self.ring[0] + self.ring[1]


class Copies:
    def __init__(self, send, recv):
        self.send, self.recv, self.made = send, recv, {}

    def put(self, name, src, dst, device):
        at = len(self.made)
        copy = pltpu.make_async_remote_copy(
            src_ref=src, dst_ref=dst, send_sem=self.send.at[at], recv_sem=self.recv.at[at],
            device_id=device, device_id_type=MESH)
        copy.start()
        self.made[name] = copy

    def got(self, name):
        self.made[name].wait_recv()

    def finish(self):
        for copy in self.made.values():
            copy.wait_send()


class Reduce:
    def __init__(self, tag, net, at, src, out, r1, p1, r2, p2, rx):
        self.tag, self.net, self.at = tag, net, at
        self.src, self.out, self.r1, self.p1, self.r2, self.p2, self.rx = src, out, r1, p1, r2, p2, rx
        self.half = src.shape[0] // 2
        self.big, self.small = self.half // 4, self.half // 16
        self.pos = ((at.y, at.z), (at.z, at.y))
        self.rings = ((at.ring[0], at.ring[1]), (at.ring[1], at.ring[0]))

    def start(self, s):
        for d in (1, 2, 3):
            to = lax.rem(self.pos[s][0] + d, 4)
            self.net.put((self.tag, 1, s, d), self.src.at[pl.ds(up16(s * self.half + to * self.big), self.big)],
                         self.r1.at[s, d - 1], self.rings[s][0][d - 1])

    def second(self, s):
        base = s * self.half + self.pos[s][0] * self.big
        for d in (1, 2, 3):
            self.net.got((self.tag, 1, s, d))
        for d in (1, 2, 3, 0):
            off = lax.rem(self.pos[s][1] + d, 4) * self.small
            rows = pl.ds(up16(off), self.small)
            total = self.src[pl.ds(up16(base + off), self.small), :].astype(F32)
            for e in range(3):
                total = total + self.r1[s, e, rows, :].astype(F32)
            self.p1[s, rows, :] = total.astype(BF16)
            if d:
                self.net.put((self.tag, 2, s, d), self.p1.at[s, rows], self.r2.at[s, d - 1], self.rings[s][1][d - 1])

    def third(self):
        for s in (0, 1):
            rows = pl.ds(up16(self.pos[s][1] * self.small), self.small)
            for d in (1, 2, 3):
                self.net.got((self.tag, 2, s, d))
            total = self.p1[s, rows, :].astype(F32)
            for e in range(3):
                total = total + self.r2[s, e].astype(F32)
            self.p2[s] = total.astype(BF16)
        self.net.put((self.tag, 3), self.p2.at[1 - self.at.xh], self.rx, self.at.far)

    def place(self, s):
        return s * self.half + self.pos[s][0] * self.big + self.pos[s][1] * self.small

    def own(self):
        self.net.got((self.tag, 3))
        where = up16(self.place(0) + self.at.xh * (self.place(1) - self.place(0)))
        rows = pl.ds(where, self.small)
        self.out[rows, :] = (self.p2[self.at.xh].astype(F32) + self.rx[...].astype(F32)).astype(BF16)
        self.net.put((self.tag, 4), self.out.at[rows], self.out.at[rows], self.at.far)

    def back(self):
        self.net.got((self.tag, 4))
        for s in (0, 1):
            rows = pl.ds(up16(self.place(s)), self.small)
            for d in (1, 2, 3):
                self.net.put((self.tag, 5, s, d), self.out.at[rows], self.out.at[rows], self.rings[s][1][d - 1])

    def spread(self):
        for s in (0, 1):
            rows = pl.ds(up16(s * self.half + self.pos[s][0] * self.big), self.big)
            for d in (1, 2, 3):
                self.net.got((self.tag, 5, s, d))
            for d in (1, 2, 3):
                self.net.put((self.tag, 6, s, d), self.out.at[rows], self.out.at[rows], self.rings[s][0][d - 1])

    def end(self):
        for s in (0, 1):
            for d in (1, 2, 3):
                self.net.got((self.tag, 6, s, d))


def column_sum8(values):
    return jnp.sum(values.reshape(values.shape[0] // 8, 8, values.shape[1]), axis=0)


S_QB, S_VB, S_OB, S_G1, S_H1, S_G2, S_H2, S_UB, S_DB, S_ROWS = 0, 2, 4, 10, 16, 22, 28, 34, 46, 64
V_OB, V_G1, V_H1, V_G2, V_H2, V_UB, V_DB = range(7)


def layer_kernel(
    length_ref, tokens, cotangent, qkv_ref, out_ref, up_ref, down_ref, vec, vec_up, qvb,
    lo_ref, ig_ref, om_ref, oa_ref, ob_ref,
    x_all, cot, normed1, n1, scale1, wown, qkvt, attt, probs, out_all, up_oth, down_oth,
    h1, n2, scale2, normed2, n2t, cott, hid, gpre, gn, gn_sib, mo, mo_sib, gh1, gb, acc, small, gattt, gt,
    g1_own, g1_sib, g1_sum, g1_far, gn1_keep, gn1_out, gn1_in, gn1_mine, gn1_far,
    gm, ga, m1, mp1, m2, mp2, mx, a1, ap1, a2, ap2, ax, send, recv,
):
    at = Place()
    i, j = at.i, at.j
    bar = pltpu.get_barrier_semaphore()
    peers = at.all()
    for peer in peers:
        pl.semaphore_signal(bar, inc=1, device_id=peer, device_id_type=MESH)
    pl.semaphore_wait(bar, len(peers))
    net = Copies(send, recv)
    mine, theirs = pl.ds(up16(256 * j), 256), pl.ds(up16(256 * (1 - j)), 256)
    ipart, opart = cols128(384 * i, 384), cols128(384 * (1 - i), 384)
    ihalf = pl.ds(up16(384 * i), 384)

    net.put("tok", tokens, x_all.at[mine], at.sib)
    net.put("cot", cotangent, cot.at[mine], at.sib)
    for n, peer in enumerate((at.xa, at.xb)):
        part = pl.ds(192 * n, 192)
        net.put(("out", n), out_ref.at[part], out_all.at[pl.ds(up16(384 * i + 192 * n), 192)], peer)
    for name, src, dst in (("up", up_ref, up_oth), ("down", down_ref, down_oth)):
        for n, peer in enumerate((at.xa, at.xb)):
            part = pl.ds(192 * n, 192)
            net.put((name, n), src.at[part], dst.at[part], peer)

    x_all[mine, :] = tokens[...]
    cot[mine, :] = cotangent[...]
    out_all[ihalf, :] = out_ref[...]
    for t in range(3):
        wown[pl.ds(192 * t, 192), :] = qkv_ref[t, pl.ds(up16(192 * j), 192), :]

    def first_norm(start):
        @pl.loop(0, 4)
        def _(b):
            rows = pl.ds(up16(start + 64 * b), 64)
            v = x_all[rows, :].astype(F32)
            c = v - jnp.mean(v, axis=-1, keepdims=True)
            sc = lax.rsqrt(jnp.mean(c * c, axis=-1, keepdims=True) + EPS)
            n = c * sc
            n1[rows, :] = n
            scale1[rows, :] = jnp.broadcast_to(sc, (64, 128))
            normed1[rows, :] = (n * vec[V_G1 : V_G1 + 1, :] + vec[V_H1 : V_H1 + 1, :]).astype(BF16)

    first_norm(256 * j)
    net.got("tok")
    first_norm(256 * (1 - j))

    for t in range(3):
        r = dot(wown[192 * t : 192 * t + 192, :], normed1[...], 1, 1)
        if t == 0:
            r = (r + qvb[0:192, :]).astype(BF16).astype(F32) * (HD**-0.5)
        if t == 2:
            r = r + qvb[192:384, :]
        qkvt[192 * t : 192 * t + 192, :] = r.astype(BF16)

    length = length_ref[0]
    own_rows = 384 * i + 192 * j
    for h in range(3):
        for qb in range(2):
            kr = 256 * (qb + 1)
            qc = slice(256 * qb, 256 * qb + 256)
            kt = qkvt[192 + 64 * h : 256 + 64 * h, 0:kr]
            s = dot(kt, qkvt[64 * h : 64 * h + 64, qc], 0, 0)
            kp = lax.broadcasted_iota(jnp.int32, (kr, 256), 0)
            qp = lax.broadcasted_iota(jnp.int32, (kr, 256), 1) + 256 * qb
            s = jnp.where((kp == qp) | ((kp < qp) & (qp < length)), s, NEG)
            e = jnp.exp(s - jnp.max(s, axis=0, keepdims=True))
            p = e * (1.0 / jnp.sum(e, axis=0, keepdims=True))
            probs[h, 0:kr, qc] = p
            o = dot(qkvt[384 + 64 * h : 448 + 64 * h, 0:kr], p.astype(BF16), 1, 0)
            attt[pl.ds(up16(own_rows + 64 * h), 64), qc] = o.astype(BF16)
        rows = pl.ds(up16(own_rows + 64 * h), 64)
        for n, peer in enumerate((at.xc, at.xa, at.sib)):
            net.put(("att", h, n), attt.at[rows], attt.at[rows], peer)

    net.got("cot")
    cott[...] = cot[:, ipart].T
    small[...] = jnp.zeros_like(small)

    def put_small(row, value):
        for c in range(value.shape[1] // 128):
            small[row + c : row + c + 1, :] = value[:, 128 * c : 128 * c + 128]

    put_small(S_DB, jnp.sum(cot[:, ipart].astype(F32), axis=0, keepdims=True))
    for n in range(2):
        net.got(("out", n))
    for h in range(3):
        for n in range(3):
            net.got(("att", h, n))

    @pl.loop(0, 4)
    def _(b):
        rows = pl.ds(up16(128 * b), 128)
        v = x_all[rows, :].astype(F32) + dot(attt[:, cols128(128 * b, 128)], out_all[...], 0, 0)
        v = v + vec[V_OB : V_OB + 1, :]
        h1[rows, :] = v
        c = v - jnp.mean(v, axis=-1, keepdims=True)
        sc = lax.rsqrt(jnp.mean(c * c, axis=-1, keepdims=True) + EPS)
        n = c * sc
        n2[rows, :] = n
        scale2[rows, :] = jnp.broadcast_to(sc, (128, 128))
        normed2[rows, :] = (n * vec[V_G2 : V_G2 + 1, :] + vec[V_H2 : V_H2 + 1, :]).astype(BF16)

    n2t[...] = normed2[:, ipart].T
    for name in ("up", "down"):
        for n in range(2):
            net.got((name, n))

    @pl.loop(0, 6)
    def _(c):
        cs = cols128(256 * c, 256)
        pre = dot(normed2[:, ipart], up_ref[:, cs], 1, 0) + dot(normed2[:, opart], up_oth[:, cs], 1, 0)
        pre = pre + vec_up[:, cs]
        g = dot(cot[:, ipart], down_ref[:, cs], 1, 0) + dot(cot[:, opart], down_oth[:, cs], 1, 0)
        k = 0.7978845608028654
        sq = pre * pre
        t = jnp.tanh(pre * (k + (k * 0.044715) * sq))
        half = 0.5 + 0.5 * t
        hid[:, cs] = (pre * half).astype(BF16)
        slope = half + (pre * half) * (1.0 - t) * (k + (3 * 0.044715 * k) * sq)
        gp = (g * slope).astype(BF16)
        gpre[:, cs] = gp
        ub = jnp.sum(gp.astype(F32), axis=0, keepdims=True)
        acc[24:25, cs] = ub

    for c in range(2):
        rows = pl.ds(256 * c, 256)
        gn[rows, ipart] = dot(gpre[rows, :], up_ref[...], 1, 1).astype(BF16)
        gn[rows, opart] = dot(gpre[rows, :], up_oth[...], 1, 1).astype(BF16)
        net.put(("gn", c), gn.at[rows], gn_sib.at[rows], at.sib)

    big = Reduce("m", net, at, gm, om_ref, m1, mp1, m2, mp2, mx)
    for s, left, right in ((1, cott, hid), (0, n2t, gpre)):
        @pl.loop(0, 6)
        def _(c):
            r = dot(left[...], right[:, cols128(256 * c, 256)], 1, 0).astype(BF16)
            for b in range(2):
                gm[pl.ds(up16(4608 * s + 384 * (2 * c + b)), 384), :] = r[:, 128 * b : 128 * b + 128]
        big.start(s)

    mo[...] = dot(hid[theirs, :], down_ref[...], 1, 1)
    net.put("mo", mo, mo_sib, at.sib)
    lo_part = dot(hid[mine, :], down_ref[...], 1, 1) + h1[mine, ipart] + vec[V_DB : V_DB + 1, 0:384]

    acc[0:24, 0:768] = jnp.zeros((24, 768), F32)
    for c in range(2):
        net.got(("gn", c))

    @pl.loop(0, 8)
    def _(b):
        rows = pl.ds(up16(64 * b), 64)
        g = gn[rows, :].astype(F32) + gn_sib[rows, :].astype(F32)
        n = n2[rows, :]
        e = g * vec[V_G2 : V_G2 + 1, :]
        m = jnp.mean(e, axis=-1, keepdims=True)
        mn = jnp.mean(e * n, axis=-1, keepdims=True)
        v = cot[rows, :].astype(F32) + (e - m - n * mn) * scale2[rows, 0:1]
        gh1[rows, :] = v
        low = v.astype(BF16)
        gb[rows, :] = low
        acc[0:8, 0:768] += column_sum8(g * n)
        acc[8:16, 0:768] += column_sum8(g)
        acc[16:24, 0:768] += column_sum8(low.astype(F32))

    put_small(S_G2, jnp.sum(acc[0:8, 0:768], axis=0, keepdims=True))
    put_small(S_H2, jnp.sum(acc[8:16, 0:768], axis=0, keepdims=True))
    put_small(S_OB, jnp.sum(acc[16:24, 0:768], axis=0, keepdims=True))
    put_small(S_UB, acc[24:25, :])

    gattt[...] = dot(out_ref[pl.ds(up16(192 * j), 192), :], gb[...], 1, 1).astype(BF16)
    net.got("mo")
    lo_ref[...] = (lo_part + mo_sib[...]).astype(BF16)

    for h in range(3):
        hs = slice(64 * h, 64 * h + 64)
        gk, gv = [], []
        for qb in range(2):
            kr = 256 * (qb + 1)
            qc = slice(256 * qb, 256 * qb + 256)
            p = probs[h, 0:kr, qc]
            gat = gattt[hs, qc]
            g = dot(qkvt[384 + 64 * h : 448 + 64 * h, 0:kr], gat, 0, 0)
            delta = jnp.sum(p * g, axis=0, keepdims=True)
            gs = (p * (g - delta)).astype(BF16)
            gt[hs, qc] = (dot(qkvt[192 + 64 * h : 256 + 64 * h, 0:kr], gs, 1, 0) * (HD**-0.5)).astype(BF16)
            gk.append(dot(qkvt[hs, qc], gs, 1, 1))
            gv.append(dot(gat, p.astype(BF16), 1, 1))
        for base, parts in ((192, gk), (384, gv)):
            rows = slice(base + 64 * h, base + 64 * h + 64)
            gt[rows, 0:256] = (parts[0] + parts[1][:, 0:256]).astype(BF16)
            gt[rows, 256:512] = parts[1][:, 256:512].astype(BF16)
        if h == 0:
            big.second(1)
            big.second(0)
        elif h == 1:
            big.third()
        else:
            big.own()

    @pl.loop(0, 2)
    def _(b):
        rows = pl.ds(up16(128 * b), 128)
        r = dot(gt[:, cols128(256 * (1 - j) + 128 * b, 128)], wown[...], 0, 0)
        gn1_out[rows, :] = r.astype(BF16)
        gn1_keep[pl.ds(up16(256 * (1 - j) + 128 * b), 128), :] = r

    net.put("gn1", gn1_out, gn1_in, at.sib)

    @pl.loop(0, 2)
    def _(b):
        r = dot(gt[:, cols128(256 * j + 128 * b, 128)], wown[...], 0, 0)
        gn1_keep[pl.ds(up16(256 * j + 128 * b), 128), :] = r

    acc[0:16, 0:768] = jnp.zeros((16, 768), F32)

    @pl.loop(0, 8)
    def _(b):
        rows = pl.ds(up16(64 * b), 64)
        g = gn1_keep[rows, :]
        acc[0:8, 0:768] += column_sum8(g * n1[rows, :])
        acc[8:16, 0:768] += column_sum8(g)

    for n in range(2):
        g1_own[8 * n : 8 * n + 8, :] = jnp.broadcast_to(
            jnp.sum(acc[8 * n : 8 * n + 8, 0:768], axis=0, keepdims=True), (8, 768))
    net.put("g1", g1_own, g1_sib, at.sib)
    big.back()

    ones = jnp.ones((16, 512), BF16)
    for base, row in ((0, S_QB), (384, S_VB)):
        r = dot(ones, gt[base : base + 192, :], 1, 1)
        small[row : row + 1, :] = r[0:1, 0:128]
        small[row + 1 : row + 2, 0:64] = r[0:1, 128:192]
    for n in range(3):
        r = dot(gt[192 * n : 192 * n + 192, :], normed1[...], 1, 0).astype(BF16)
        for c in range(6):
            ga[pl.ds(576 * c + 192 * n, 192), :] = r[:, 128 * c : 128 * c + 128]
    r = dot(attt[pl.ds(up16(own_rows), 192), :], gb[...], 1, 0).astype(BF16)
    for c in range(6):
        ga[pl.ds(3456 + 192 * c, 192), :] = r[:, 128 * c : 128 * c + 128]
    ga[pl.ds(4608 + S_ROWS, 512 - S_ROWS), :] = jnp.zeros((512 - S_ROWS, 128), BF16)
    tail = Reduce("a", net, at, ga, oa_ref, a1, ap1, a2, ap2, ax)
    tail.start(0)

    net.got("g1")
    g1_sum[...] = g1_own[...] + g1_sib[...]
    net.put("g1x", g1_sum, g1_far, at.xa)
    net.got("gn1")
    half_sum = gn1_keep[mine, :] + gn1_in[...].astype(F32)
    gn1_mine[...] = half_sum.astype(BF16)
    net.put("gn1x", gn1_mine, gn1_far, at.xa)
    net.got("g1x")
    g1_own_sum = g1_sum[...] + g1_far[...]
    put_small(S_G1, g1_own_sum[0:1, :])
    put_small(S_H1, g1_own_sum[8:9, :])
    ga[pl.ds(4608, S_ROWS), :] = small[...].astype(BF16)
    tail.start(1)
    big.spread()
    tail.second(0)
    tail.second(1)
    tail.third()
    net.got("gn1x")

    @pl.loop(0, 4)
    def _(b):
        rows = pl.ds(up16(64 * b), 64)
        full = pl.ds(up16(256 * j + 64 * b), 64)
        g = gn1_mine[rows, :].astype(F32) + gn1_far[rows, :].astype(F32)
        n = n1[full, :]
        e = g * vec[V_G1 : V_G1 + 1, :]
        m = jnp.mean(e, axis=-1, keepdims=True)
        mn = jnp.mean(e * n, axis=-1, keepdims=True)
        ig_ref[rows, :] = gh1[full, :] + (e - m - n * mn) * scale1[full, 0:1]

    tail.own()
    tail.back()
    tail.spread()
    big.end()
    tail.end()
    net.put("sib", oa_ref, ob_ref, at.sib)
    net.got("sib")
    net.finish()


def layer_call(length, tokens, cotangent, qkv, out_w, up_w, down_w, vec, vec_up, qvb):
    V = pltpu.VMEM
    sds = jax.ShapeDtypeStruct
    scratch = [
        V((512, 768), BF16), V((512, 768), BF16), V((512, 768), BF16), V((512, 768), F32), V((512, 128), F32),
        V((576, 768), BF16), V((576, 512), BF16), V((768, 512), BF16), V((3, 512, 512), F32), V((768, 768), BF16),
        V((384, 1536), BF16), V((384, 1536), BF16),
        V((512, 768), F32), V((512, 768), F32), V((512, 128), F32), V((512, 768), BF16), V((384, 512), BF16),
        V((384, 512), BF16), V((512, 1536), BF16), V((512, 1536), BF16), V((512, 768), BF16), V((512, 768), BF16),
        V((256, 384), F32), V((256, 384), F32), V((512, 768), F32), V((512, 768), BF16), V((32, 1536), F32),
        V((S_ROWS, 128), F32), V((192, 512), BF16), V((576, 512), BF16),
        V((16, 768), F32), V((16, 768), F32), V((16, 768), F32), V((16, 768), F32),
        V((512, 768), F32), V((256, 768), BF16), V((256, 768), BF16), V((256, 768), BF16), V((256, 768), BF16),
        V((9216, 128), BF16), V((5120, 128), BF16),
        V((2, 3, 1152, 128), BF16), V((2, 1152, 128), BF16), V((2, 3, 288, 128), BF16), V((2, 288, 128), BF16), V((288, 128), BF16),
        V((2, 3, 640, 128), BF16), V((2, 640, 128), BF16), V((2, 3, 160, 128), BF16), V((2, 160, 128), BF16), V((160, 128), BF16),
        pltpu.SemaphoreType.DMA((96,)), pltpu.SemaphoreType.DMA((96,)),
    ]
    vm = pl.BlockSpec(memory_space=V)
    return pl.pallas_call(
        layer_kernel,
        out_shape=(sds((256, 384), BF16), sds((256, 768), F32), sds((9216, 128), BF16), sds((5120, 128), BF16),
                   sds((5120, 128), BF16)),
        in_specs=[pl.BlockSpec(memory_space=pltpu.SMEM)] + [vm] * 9,
        out_specs=(vm,) * 5,
        scratch_shapes=scratch,
        compiler_params=pltpu.CompilerParams(collective_id=0, has_side_effects=True, vmem_limit_bytes=60 << 20),
        name="layer",
    )(length, tokens, cotangent, qkv, out_w, up_w, down_w, vec, vec_up, qvb)


def per_device(tokens, seq_lengths, cotangent, qkv_weight, qv_bias, out_weight, out_bias,
               first_gain, first_shift, second_gain, second_shift, up_weight, up_bias, down_weight, down_bias):
    j = lax.axis_index("grid")
    own = lax.dynamic_slice_in_dim(qv_bias, 192 * j, 192, 1)
    qvb = jnp.broadcast_to(own.reshape(384, 1), (384, 512))
    rows = [out_bias, first_gain, first_shift, second_gain, second_shift, jnp.zeros_like(out_bias),
            jnp.pad(down_bias, (0, 384)), jnp.zeros_like(out_bias)]
    lo, ig, om, oa, ob = layer_call(
        seq_lengths, tokens, cotangent, qkv_weight, out_weight, up_weight, down_weight,
        jnp.stack(rows), up_bias.reshape(1, -1), qvb)
    return finish(lo, ig, om, oa, ob, j)


def finish(lo, ig, om, oa, ob, j):
    first = jnp.where(j == 0, oa, ob).astype(F32)
    second = jnp.where(j == 0, ob, oa).astype(F32)
    mlp = om.astype(F32).reshape(2, 12, 384, 128).transpose(0, 2, 1, 3).reshape(2, 384, 1536)
    qkv = [a[:3456].reshape(6, 3, 192, 128).transpose(1, 2, 0, 3).reshape(3, 192, 768) for a in (first, second)]
    outw = [a[3456:4608].reshape(6, 192, 128).transpose(1, 0, 2).reshape(192, 768) for a in (first, second)]
    sm = oa[4608 : 4608 + S_ROWS].astype(F32)
    bias = [a[4608 : 4608 + 4].reshape(2, 256)[:, :192] for a in (first, second)]
    row = lambda at, n: sm[at : at + n].reshape(-1)
    return (
        lo, ig, jnp.concatenate(qkv, axis=1), jnp.concatenate(bias, axis=1), jnp.concatenate(outw, axis=0),
        row(S_OB, 6), row(S_G1, 6), row(S_H1, 6), row(S_G2, 6), row(S_H2, 6),
        mlp[0], row(S_UB, 12), mlp[1], row(S_DB, 3),
    )
def solution(mesh):
    placed = (
        P(("dp", "grid"), None), P("dp"), P(("dp", "grid"), None), P(None, "mp", None), P(None, "mp"),
        P("mp", None), P(), P(), P(), P(), P(), P("mp", "grid"), P("grid"), P("mp", "grid"), P("mp"),
    )
    return jax.shard_map(
        per_device,
        mesh=mesh,
        in_specs=placed,
        out_specs=(
            P(("dp", "grid"), "mp"), P(("dp", "grid"), None), P(None, "mp", None), P(None, "mp"), P("mp", None),
            P(), P(), P(), P(), P(), P("mp", "grid"), P("grid"), P("mp", "grid"), P("mp"),
        ),
        check_vma=False,
    )
```

```python
import functools

import jax
import jax.numpy as jnp
from jax import lax
from jax.experimental import pallas as pl
from jax.experimental.pallas import tpu as pltpu
from jax.sharding import PartitionSpec as P

HD = 64
EPS = 1e-05
NEG = -1e30
MESH = pl.DeviceIdType.MESH
F32, BF16 = jnp.float32, jnp.bfloat16


def dot(left, right, left_dim, right_dim):
    return lax.dot_general(
        left, right, (((left_dim,), (right_dim,)), ((), ())), preferred_element_type=F32
    )


def up16(value):
    return pl.multiple_of(value, 16)


def cols128(start, size):
    return pl.ds(pl.multiple_of(start, 128), size)


class Place:
    def __init__(self):
        dp = lax.axis_index("dp")
        self.i, self.j = lax.axis_index("mp"), lax.axis_index("grid")
        self.xh, self.y, self.z = lax.rem(dp, 2), lax.rem(lax.div(dp, 2), 4), lax.div(dp, 8)
        self.sib = {"grid": 1 - self.j}
        self.xa = {"mp": 1 - self.i}
        self.xb = {"dp": dp + 1 - 2 * self.xh, "mp": 1 - self.i}
        self.xc = {"mp": 1 - self.i, "grid": 1 - self.j}
        steps = (
            [2 * (lax.rem(self.y + d, 4) - self.y) for d in range(4)],
            [8 * (lax.rem(self.z + d, 4) - self.z) for d in range(4)],
        )
        flip = [0, 1 - 2 * self.xh]
        self.ring = [[{"dp": dp + r[d]} for d in (1, 2, 3)] for r in steps]
        self.eight = [[{"dp": dp + r[k // 2] + flip[k % 2]} for k in range(8)] for r in steps]

    def all(self):
        return [self.sib, self.xa, self.xb, self.xc] + self.eight[0][1:] + self.eight[1][2:]


class Copies:
    def __init__(self, send, recv):
        self.send, self.recv, self.made = send, recv, {}

    def put(self, name, src, dst, device):
        at = len(self.made)
        copy = pltpu.make_async_remote_copy(
            src_ref=src, dst_ref=dst, send_sem=self.send.at[at], recv_sem=self.recv.at[at],
            device_id=device, device_id_type=MESH)
        copy.start()
        self.made[name] = copy

    def got(self, name):
        self.made[name].wait_recv()

    def finish(self):
        for copy in self.made.values():
            copy.wait_send()


class Reduce:
    def __init__(self, tag, net, at, src, out, r1, p1, r2):
        self.tag, self.net, self.at = tag, net, at
        self.src, self.out, self.r1, self.p1, self.r2 = src, out, r1, p1, r2
        self.half = src.shape[0] // 2
        self.big, self.small = self.half // 4, self.half // 32
        self.pos = ((at.y, at.z), (at.z, at.y))
        self.rings = ((at.ring[0],), (at.ring[1],))
        self.eights = (at.eight[1], at.eight[0])

    def start(self, s):
        for d in (1, 2, 3):
            to = lax.rem(self.pos[s][0] + d, 4)
            self.net.put((self.tag, 1, s, d), self.src.at[pl.ds(up16(s * self.half + to * self.big), self.big)],
                         self.r1.at[s, d - 1], self.rings[s][0][d - 1])

    def part(self, s, k):
        across = self.at.xh + (k % 2) * (1 - 2 * self.at.xh)
        return (2 * lax.rem(self.pos[s][1] + k // 2, 4) + across) * self.small

    def second(self, s):
        base = s * self.half + self.pos[s][0] * self.big
        for d in (1, 2, 3):
            self.net.got((self.tag, 1, s, d))
        for k in (1, 2, 3, 4, 5, 6, 7, 0):
            off = self.part(s, k)
            rows = pl.ds(up16(off), self.small)
            total = self.src[pl.ds(up16(base + off), self.small), :].astype(F32)
            for e in range(3):
                total = total + self.r1[s, e, rows, :].astype(F32)
            self.p1[s, rows, :] = total.astype(BF16)
            if k:
                self.net.put((self.tag, 2, s, k), self.p1.at[s, rows], self.r2.at[s, k - 1], self.eights[s][k])

    def place(self, s):
        return pl.ds(up16(s * self.half + self.pos[s][0] * self.big + self.part(s, 0)), self.small)

    def own(self, s):
        for k in range(1, 8):
            self.net.got((self.tag, 2, s, k))
        total = self.p1[s, pl.ds(up16(self.part(s, 0)), self.small), :].astype(F32)
        for e in range(7):
            total = total + self.r2[s, e].astype(F32)
        rows = self.place(s)
        self.out[rows, :] = total.astype(BF16)
        for k in range(1, 8):
            self.net.put((self.tag, 3, s, k), self.out.at[rows], self.out.at[rows], self.eights[s][k])

    def spread(self, s):
        rows = pl.ds(up16(s * self.half + self.pos[s][0] * self.big), self.big)
        for k in range(1, 8):
            self.net.got((self.tag, 3, s, k))
        for d in (1, 2, 3):
            self.net.put((self.tag, 4, s, d), self.out.at[rows], self.out.at[rows], self.rings[s][0][d - 1])

    def end(self):
        for s in (0, 1):
            for d in (1, 2, 3):
                self.net.got((self.tag, 4, s, d))


def column_sum8(values):
    return jnp.sum(values.reshape(values.shape[0] // 8, 8, values.shape[1]), axis=0)


S_QB, S_VB, S_OB, S_G1, S_H1, S_G2, S_H2, S_UB, S_DB, S_ROWS = 0, 2, 4, 10, 16, 22, 28, 34, 46, 64
V_OB, V_G1, V_H1, V_G2, V_H2, V_UB, V_DB = range(7)


def layer_kernel(
    length_ref, tokens, cotangent, qkv_ref, out_ref, up_ref, down_ref, qvb_in, ob_in, g1_in, h1_in, g2_in, h2_in,
    ub_in, db_in,
    lo_ref, ig_ref, om_ref, oa_ref, ob_ref,
    x_all, cot, normed1, n1, scale1, wown, qkvt, attt, probs, out_all, up_oth, down_oth,
    h1, n2, scale2, normed2, n2t, cott, hid, gpre, gn, gn_sib, mo, mo_sib, gh1, gb, acc, small, gattt, gt,
    g1_own, g1_sib, g1_sum, g1_far, gn1_keep, gn1_out, gn1_in, gn1_mine, gn1_far,
    gm, ga, m1, mp1, m2, a1, ap1, a2, vec, vec_up, send, recv,
):
    at = Place()
    i, j = at.i, at.j
    bar = pltpu.get_barrier_semaphore()
    peers = at.all()
    for peer in peers:
        pl.semaphore_signal(bar, inc=1, device_id=peer, device_id_type=MESH)
    pl.semaphore_wait(bar, len(peers))
    net = Copies(send, recv)
    mine, theirs = pl.ds(up16(256 * j), 256), pl.ds(up16(256 * (1 - j)), 256)
    ipart, opart = cols128(384 * i, 384), cols128(384 * (1 - i), 384)
    ihalf = pl.ds(up16(384 * i), 384)

    net.put("tok", tokens, x_all.at[mine], at.sib)
    net.put("cot", cotangent, cot.at[mine], at.sib)
    for n, peer in enumerate((at.xa, at.xb)):
        part = 192 * j + 96 * n
        net.put(("out", n), out_ref.at[pl.ds(up16(part), 96)], out_all.at[pl.ds(up16(384 * i + part), 96)], peer)
    odd_y, odd_z = lax.rem(at.y, 2), lax.rem(at.z, 2)
    quarter = 2 * odd_y + odd_z
    weights = (("up", up_ref, up_oth), ("down", down_ref, down_oth))

    def weight_rows(q, n):
        return pl.ds(up16(96 * q + 48 * n), 48)

    for way, q in (("x", quarter), ("w", 3 - quarter)):
        for name, src, dst in weights:
            for n, peer in enumerate((at.xa, at.xb)):
                net.put((name, way, n), src.at[weight_rows(q, n)], dst.at[weight_rows(q, n)], peer)

    def pass_on(which):
        name, _, dst = weights[which]
        for n in range(2):
            net.got((name, "x", n))
        for axis in range(2):
            for n in range(2):
                rows = weight_rows(quarter, n)
                net.put((name, axis, n), dst.at[rows], dst.at[rows], at.ring[axis][2 * n])

    def weight_here(which):
        name = weights[which][0]
        for way in ("w", 0, 1):
            for n in range(2):
                net.got((name, way, n))

    x_all[mine, :] = tokens[...]
    cot[mine, :] = cotangent[...]
    out_all[ihalf, :] = out_ref[...]
    for t in range(3):
        wown[pl.ds(192 * t, 192), :] = qkv_ref[t, pl.ds(up16(192 * j), 192), :]

    def first_norm(start):
        @pl.loop(0, 4)
        def _(b):
            rows = pl.ds(up16(start + 64 * b), 64)
            v = x_all[rows, :].astype(F32)
            c = v - jnp.mean(v, axis=-1, keepdims=True)
            sc = lax.rsqrt(jnp.mean(c * c, axis=-1, keepdims=True) + EPS)
            n = c * sc
            n1[rows, :] = n
            scale1[rows, :] = jnp.broadcast_to(sc, (64, 128))
            normed1[rows, :] = (n * vec[V_G1 : V_G1 + 1, :] + vec[V_H1 : V_H1 + 1, :]).astype(BF16)

    for n, ref in enumerate((ob_in, g1_in, h1_in, g2_in, h2_in)):
        vec[n : n + 1, :] = ref[...].reshape(1, 768)
    vec[V_DB : V_DB + 1, 0:384] = db_in[...].reshape(1, 384)
    vec_up[...] = ub_in[...].reshape(1, 1536)
    first_norm(256 * j)
    net.got("tok")
    first_norm(256 * (1 - j))

    ones = jnp.ones((16, 512), BF16)
    line = lax.broadcasted_iota(jnp.int32, (16, 192), 0)

    def bias_columns(n):
        b = jnp.where(j == 0, qvb_in[n : n + 1, 0:192], qvb_in[n : n + 1, 192:384])
        t1 = b.astype(BF16).astype(F32)
        t2 = (b - t1).astype(BF16).astype(F32)
        terms = jnp.where(line == 0, t1, jnp.where(line == 1, t2, jnp.where(line == 2, b - t1 - t2, 0.0)))
        return dot(terms.astype(BF16), ones, 0, 0)

    for t in range(3):
        r = dot(wown[192 * t : 192 * t + 192, :], normed1[...], 1, 1)
        if t == 0:
            r = (r + bias_columns(0)).astype(BF16).astype(F32) * (HD**-0.5)
        if t == 2:
            r = r + bias_columns(1)
        qkvt[192 * t : 192 * t + 192, :] = r.astype(BF16)

    pass_on(0)
    length = length_ref[0]
    own_rows = 384 * i + 192 * j
    for h in range(3):
        for qb in range(2):
            kr = 256 * (qb + 1)
            qc = slice(256 * qb, 256 * qb + 256)
            kt = qkvt[192 + 64 * h : 256 + 64 * h, 0:kr]
            s = dot(kt, qkvt[64 * h : 64 * h + 64, qc], 0, 0)
            kp = lax.broadcasted_iota(jnp.int32, (kr, 256), 0)
            qp = lax.broadcasted_iota(jnp.int32, (kr, 256), 1) + 256 * qb
            s = jnp.where((kp == qp) | ((kp < qp) & (qp < length)), s, NEG)
            e = jnp.exp(s - jnp.max(s, axis=0, keepdims=True))
            p = e * (1.0 / jnp.sum(e, axis=0, keepdims=True))
            probs[h, 0:kr, qc] = p
            o = dot(qkvt[384 + 64 * h : 448 + 64 * h, 0:kr], p.astype(BF16), 1, 0)
            attt[pl.ds(up16(own_rows + 64 * h), 64), qc] = o.astype(BF16)
        rows = pl.ds(up16(own_rows + 64 * h), 64)
        for n, peer in enumerate((at.xc, at.xa, at.sib)):
            net.put(("att", h, n), attt.at[rows], attt.at[rows], peer)
        if h == 0:
            pass_on(1)
        if h == 1:
            for n in range(2):
                net.got(("out", n))
            far_rows = pl.ds(up16(384 * (1 - i) + 192 * j), 192)
            net.put("outs", out_all.at[far_rows], out_all.at[far_rows], at.sib)

    net.got("cot")
    cott[...] = cot[:, ipart].T
    small[...] = jnp.zeros_like(small)

    def put_small(row, value):
        for c in range(value.shape[1] // 128):
            small[row + c : row + c + 1, :] = value[:, 128 * c : 128 * c + 128]

    put_small(S_DB, jnp.sum(cot[:, ipart].astype(F32), axis=0, keepdims=True))
    net.got("outs")
    for h in range(3):
        for n in range(3):
            net.got(("att", h, n))

    @pl.loop(0, 4)
    def _(b):
        rows = pl.ds(up16(128 * b), 128)
        v = x_all[rows, :].astype(F32) + dot(attt[:, cols128(128 * b, 128)], out_all[...], 0, 0)
        v = v + vec[V_OB : V_OB + 1, :]
        h1[rows, :] = v
        c = v - jnp.mean(v, axis=-1, keepdims=True)
        sc = lax.rsqrt(jnp.mean(c * c, axis=-1, keepdims=True) + EPS)
        n = c * sc
        n2[rows, :] = n
        scale2[rows, :] = jnp.broadcast_to(sc, (128, 128))
        normed2[rows, :] = (n * vec[V_G2 : V_G2 + 1, :] + vec[V_H2 : V_H2 + 1, :]).astype(BF16)

    n2t[...] = normed2[:, ipart].T
    weight_here(0)
    weight_here(1)

    @pl.loop(0, 6)
    def _(c):
        cs = cols128(256 * c, 256)
        pre = dot(normed2[:, ipart], up_ref[:, cs], 1, 0) + dot(normed2[:, opart], up_oth[:, cs], 1, 0)
        pre = pre + vec_up[:, cs]
        g = dot(cot[:, ipart], down_ref[:, cs], 1, 0) + dot(cot[:, opart], down_oth[:, cs], 1, 0)
        k = 0.7978845608028654
        sq = pre * pre
        t = jnp.tanh(pre * (k + (k * 0.044715) * sq))
        half = 0.5 + 0.5 * t
        hid[:, cs] = (pre * half).astype(BF16)
        slope = half + (pre * half) * (1.0 - t) * (k + (3 * 0.044715 * k) * sq)
        gp = (g * slope).astype(BF16)
        gpre[:, cs] = gp
        ub = jnp.sum(gp.astype(F32), axis=0, keepdims=True)
        acc[24:25, cs] = ub

    for c in range(2):
        rows = pl.ds(256 * c, 256)
        gn[rows, ipart] = dot(gpre[rows, :], up_ref[...], 1, 1).astype(BF16)
        gn[rows, opart] = dot(gpre[rows, :], up_oth[...], 1, 1).astype(BF16)
        net.put(("gn", c), gn.at[rows], gn_sib.at[rows], at.sib)

    big = Reduce("m", net, at, gm, om_ref, m1, mp1, m2)
    for s, left, right in ((1, cott, hid), (0, n2t, gpre)):
        @pl.loop(0, 6)
        def _(c):
            r = dot(left[...], right[:, cols128(256 * c, 256)], 1, 0).astype(BF16)
            for b in range(2):
                gm[pl.ds(up16(4608 * s + 384 * (2 * c + b)), 384), :] = r[:, 128 * b : 128 * b + 128]
        big.start(s)

    mo[...] = dot(hid[theirs, :], down_ref[...], 1, 1)
    net.put("mo", mo, mo_sib, at.sib)
    lo_part = dot(hid[mine, :], down_ref[...], 1, 1) + h1[mine, ipart] + vec[V_DB : V_DB + 1, 0:384]

    acc[0:24, 0:768] = jnp.zeros((24, 768), F32)
    for c in range(2):
        net.got(("gn", c))

    @pl.loop(0, 8)
    def _(b):
        rows = pl.ds(up16(64 * b), 64)
        g = gn[rows, :].astype(F32) + gn_sib[rows, :].astype(F32)
        n = n2[rows, :]
        e = g * vec[V_G2 : V_G2 + 1, :]
        m = jnp.mean(e, axis=-1, keepdims=True)
        mn = jnp.mean(e * n, axis=-1, keepdims=True)
        v = cot[rows, :].astype(F32) + (e - m - n * mn) * scale2[rows, 0:1]
        gh1[rows, :] = v
        low = v.astype(BF16)
        gb[rows, :] = low
        acc[0:8, 0:768] += column_sum8(g * n)
        acc[8:16, 0:768] += column_sum8(g)
        acc[16:24, 0:768] += column_sum8(low.astype(F32))

    put_small(S_G2, jnp.sum(acc[0:8, 0:768], axis=0, keepdims=True))
    put_small(S_H2, jnp.sum(acc[8:16, 0:768], axis=0, keepdims=True))
    put_small(S_OB, jnp.sum(acc[16:24, 0:768], axis=0, keepdims=True))
    put_small(S_UB, acc[24:25, :])

    gattt[...] = dot(out_ref[pl.ds(up16(192 * j), 192), :], gb[...], 1, 1).astype(BF16)
    net.got("mo")
    lo_ref[...] = (lo_part + mo_sib[...]).astype(BF16)

    for h in range(3):
        hs = slice(64 * h, 64 * h + 64)
        gk, gv = [], []
        for qb in range(2):
            kr = 256 * (qb + 1)
            qc = slice(256 * qb, 256 * qb + 256)
            p = probs[h, 0:kr, qc]
            gat = gattt[hs, qc]
            g = dot(qkvt[384 + 64 * h : 448 + 64 * h, 0:kr], gat, 0, 0)
            delta = jnp.sum(p * g, axis=0, keepdims=True)
            gs = (p * (g - delta)).astype(BF16)
            gt[hs, qc] = (dot(qkvt[192 + 64 * h : 256 + 64 * h, 0:kr], gs, 1, 0) * (HD**-0.5)).astype(BF16)
            gk.append(dot(qkvt[hs, qc], gs, 1, 1))
            gv.append(dot(gat, p.astype(BF16), 1, 1))
        for base, parts in ((192, gk), (384, gv)):
            rows = slice(base + 64 * h, base + 64 * h + 64)
            gt[rows, 0:256] = (parts[0] + parts[1][:, 0:256]).astype(BF16)
            gt[rows, 256:512] = parts[1][:, 256:512].astype(BF16)
        if h == 1:
            big.second(1)
        if h == 2:
            big.second(0)

    @pl.loop(0, 2)
    def _(b):
        rows = pl.ds(up16(128 * b), 128)
        r = dot(gt[:, cols128(256 * (1 - j) + 128 * b, 128)], wown[...], 0, 0)
        gn1_out[rows, :] = r.astype(BF16)
        gn1_keep[pl.ds(up16(256 * (1 - j) + 128 * b), 128), :] = r

    net.put("gn1", gn1_out, gn1_in, at.sib)

    @pl.loop(0, 2)
    def _(b):
        r = dot(gt[:, cols128(256 * j + 128 * b, 128)], wown[...], 0, 0)
        gn1_keep[pl.ds(up16(256 * j + 128 * b), 128), :] = r

    acc[0:16, 0:768] = jnp.zeros((16, 768), F32)

    @pl.loop(0, 8)
    def _(b):
        rows = pl.ds(up16(64 * b), 64)
        g = gn1_keep[rows, :]
        acc[0:8, 0:768] += column_sum8(g * n1[rows, :])
        acc[8:16, 0:768] += column_sum8(g)

    for n in range(2):
        g1_own[8 * n : 8 * n + 8, :] = jnp.broadcast_to(
            jnp.sum(acc[8 * n : 8 * n + 8, 0:768], axis=0, keepdims=True), (8, 768))
    net.put("g1", g1_own, g1_sib, at.sib)
    big.own(1)

    for base, row in ((0, S_QB), (384, S_VB)):
        r = dot(ones, gt[base : base + 192, :], 1, 1)
        small[row : row + 1, :] = r[0:1, 0:128]
        small[row + 1 : row + 2, 0:64] = r[0:1, 128:192]
    net.got("g1")
    g1_sum[...] = g1_own[...] + g1_sib[...]
    net.put("g1x", g1_sum, g1_far, at.xa)
    net.got("gn1")
    half_sum = gn1_keep[mine, :] + gn1_in[...].astype(F32)
    gn1_mine[...] = half_sum.astype(BF16)
    net.put("gn1x", gn1_mine, gn1_far, at.xa)
    big.own(0)
    for n in range(3):
        r = dot(gt[192 * n : 192 * n + 192, :], normed1[...], 1, 0).astype(BF16)
        for c in range(6):
            ga[pl.ds(576 * c + 192 * n, 192), :] = r[:, 128 * c : 128 * c + 128]
    r = dot(attt[pl.ds(up16(own_rows), 192), :], gb[...], 1, 0).astype(BF16)
    for c in range(6):
        ga[pl.ds(3456 + 192 * c, 192), :] = r[:, 128 * c : 128 * c + 128]
    ga[pl.ds(4608 + S_ROWS, 512 - S_ROWS), :] = jnp.zeros((512 - S_ROWS, 128), BF16)
    tail = Reduce("a", net, at, ga, oa_ref, a1, ap1, a2)
    tail.start(0)

    net.got("g1x")
    g1_own_sum = g1_sum[...] + g1_far[...]
    put_small(S_G1, g1_own_sum[0:1, :])
    put_small(S_H1, g1_own_sum[8:9, :])
    ga[pl.ds(4608, S_ROWS), :] = small[...].astype(BF16)
    tail.start(1)
    big.spread(1)
    big.spread(0)
    tail.second(0)
    tail.second(1)
    net.got("gn1x")

    @pl.loop(0, 4)
    def _(b):
        rows = pl.ds(up16(64 * b), 64)
        full = pl.ds(up16(256 * j + 64 * b), 64)
        g = gn1_mine[rows, :].astype(F32) + gn1_far[rows, :].astype(F32)
        n = n1[full, :]
        e = g * vec[V_G1 : V_G1 + 1, :]
        m = jnp.mean(e, axis=-1, keepdims=True)
        mn = jnp.mean(e * n, axis=-1, keepdims=True)
        ig_ref[rows, :] = gh1[full, :] + (e - m - n * mn) * scale1[full, 0:1]

    tail.own(0)
    tail.own(1)
    tail.spread(0)
    tail.spread(1)
    big.end()
    tail.end()
    net.put("sib", oa_ref, ob_ref, at.sib)
    net.got("sib")
    net.finish()


def layer_call(*args):
    V = pltpu.VMEM
    sds = jax.ShapeDtypeStruct
    scratch = [
        V((512, 768), BF16), V((512, 768), BF16), V((512, 768), BF16), V((512, 768), F32), V((512, 128), F32),
        V((576, 768), BF16), V((576, 512), BF16), V((768, 512), BF16), V((3, 512, 512), F32), V((768, 768), BF16),
        V((384, 1536), BF16), V((384, 1536), BF16),
        V((512, 768), F32), V((512, 768), F32), V((512, 128), F32), V((512, 768), BF16), V((384, 512), BF16),
        V((384, 512), BF16), V((512, 1536), BF16), V((512, 1536), BF16), V((512, 768), BF16), V((512, 768), BF16),
        V((256, 384), F32), V((256, 384), F32), V((512, 768), F32), V((512, 768), BF16), V((32, 1536), F32),
        V((S_ROWS, 128), F32), V((192, 512), BF16), V((576, 512), BF16),
        V((16, 768), F32), V((16, 768), F32), V((16, 768), F32), V((16, 768), F32),
        V((512, 768), F32), V((256, 768), BF16), V((256, 768), BF16), V((256, 768), BF16), V((256, 768), BF16),
        V((9216, 128), BF16), V((5120, 128), BF16),
        V((2, 3, 1152, 128), BF16), V((2, 1152, 128), BF16), V((2, 7, 144, 128), BF16),
        V((2, 3, 640, 128), BF16), V((2, 640, 128), BF16), V((2, 7, 80, 128), BF16),
        V((8, 768), F32), V((1, 1536), F32),
        pltpu.SemaphoreType.DMA((160,)), pltpu.SemaphoreType.DMA((160,)),
    ]
    vm = pl.BlockSpec(memory_space=V)
    return pl.pallas_call(
        layer_kernel,
        out_shape=(sds((256, 384), BF16), sds((256, 768), F32), sds((9216, 128), BF16), sds((5120, 128), BF16),
                   sds((5120, 128), BF16)),
        in_specs=[pl.BlockSpec(memory_space=pltpu.SMEM)] + [vm] * 14,
        out_specs=(vm,) * 5,
        scratch_shapes=scratch,
        compiler_params=pltpu.CompilerParams(collective_id=0, has_side_effects=True, vmem_limit_bytes=60 << 20),
        name="layer",
    )(*args)


def finish_kernel(lo, ig, om, oa, ob, lo_out, ig_out, qkv_out, qvb_out, ow_out, out_bias, gain1, shift1, gain2, shift2,
                  up_out, up_bias, down_out, down_bias, qkv, ow, up, down, sems):
    j = lax.axis_index("grid")
    copies = []

    def send(src, dst):
        copy = pltpu.make_async_copy(src, dst, sems.at[len(copies)])
        copy.start()
        copies.append(copy)

    send(lo, lo_out)
    send(ig, ig_out)
    for s, scr, dst in ((0, up, up_out), (1, down, down_out)):
        for c in range(12):
            scr[:, 128 * c : 128 * c + 128] = om[4608 * s + 384 * c : 4608 * s + 384 * c + 384, :].astype(F32)
        send(scr, dst)
    for src, side in ((oa, j), (ob, 1 - j)):
        rows = pl.ds(pl.multiple_of(192 * side, 192), 192)
        for c in range(6):
            ow[rows, 128 * c : 128 * c + 128] = src[3456 + 192 * c : 3648 + 192 * c, :].astype(F32)
    send(ow, ow_out)
    for n in range(3):
        for src, side in ((oa, j), (ob, 1 - j)):
            rows = pl.ds(pl.multiple_of(192 * side, 192), 192)
            for c in range(6):
                at = 576 * c + 192 * n
                qkv[n, rows, 128 * c : 128 * c + 128] = src[at : at + 192, :].astype(F32)
        send(qkv.at[n], qkv_out.at[n])
    mine, other = (a[4608 : 4608 + S_ROWS, :].astype(F32) for a in (oa, ob))
    first, second = jnp.where(j == 0, mine, other), jnp.where(j == 0, other, mine)
    for n in range(2):
        qvb_out[n : n + 1, :] = jnp.concatenate(
            [part[2 * n + c : 2 * n + c + 1, : 128 - 64 * c] for part in (first, second) for c in range(2)], axis=1)
    for dst, row, count in ((out_bias, S_OB, 6), (gain1, S_G1, 6), (shift1, S_H1, 6), (gain2, S_G2, 6),
                            (shift2, S_H2, 6), (up_bias, S_UB, 12), (down_bias, S_DB, 3)):
        for c in range(count):
            dst[128 * c : 128 * c + 128] = mine[row + c]
    for copy in copies:
        copy.wait()


def finish(*args):
    V, hbm = pl.BlockSpec(memory_space=pltpu.VMEM), pl.BlockSpec(memory_space=pl.ANY)
    f = lambda *shape: jax.ShapeDtypeStruct(shape, F32)
    return pl.pallas_call(
        finish_kernel,
        out_shape=(jax.ShapeDtypeStruct((256, 384), BF16), f(256, 768), f(3, 384, 768), f(2, 384), f(384, 768),
                   f(768), f(768), f(768), f(768), f(768), f(384, 1536), f(1536), f(384, 1536), f(384)),
        in_specs=[hbm, hbm, V, V, V],
        out_specs=(hbm, hbm, hbm, V, hbm, V, V, V, V, V, hbm, V, hbm, V),
        scratch_shapes=[pltpu.VMEM((3, 384, 768), F32), pltpu.VMEM((384, 768), F32), pltpu.VMEM((384, 1536), F32),
                        pltpu.VMEM((384, 1536), F32), pltpu.SemaphoreType.DMA((8,))],
        compiler_params=pltpu.CompilerParams(vmem_limit_bytes=40 << 20),
        name="finish",
    )(*args)


def per_device(tokens, seq_lengths, cotangent, qkv_weight, qv_bias, out_weight, out_bias,
               first_gain, first_shift, second_gain, second_shift, up_weight, up_bias, down_weight, down_bias):
    return finish(*layer_call(
        seq_lengths, tokens, cotangent, qkv_weight, out_weight, up_weight, down_weight, qv_bias, out_bias,
        first_gain, first_shift, second_gain, second_shift, up_bias, down_bias))


def solution(mesh):
    placed = (
        P(("dp", "grid"), None), P("dp"), P(("dp", "grid"), None), P(None, "mp", None), P(None, "mp"),
        P("mp", None), P(), P(), P(), P(), P(), P("mp", "grid"), P("grid"), P("mp", "grid"), P("mp"),
    )
    return jax.shard_map(
        per_device,
        mesh=mesh,
        in_specs=placed,
        out_specs=(
            P(("dp", "grid"), "mp"), P(("dp", "grid"), None), P(None, "mp", None), P(None, "mp"), P("mp", None),
            P(), P(), P(), P(), P(), P("mp", "grid"), P("grid"), P("mp", "grid"), P("mp"),
        ),
        check_vma=False,
    )
```

```python
import functools

import jax
import jax.numpy as jnp
from jax import lax
from jax.experimental import pallas as pl
from jax.experimental.pallas import tpu as pltpu
from jax.sharding import PartitionSpec as P

HD = 64
EPS = 1e-05
NEG = -1e30
MESH = pl.DeviceIdType.MESH
F32, BF16 = jnp.float32, jnp.bfloat16


def dot(left, right, left_dim, right_dim):
    return lax.dot_general(
        left, right, (((left_dim,), (right_dim,)), ((), ())), preferred_element_type=F32
    )


def up16(value):
    return pl.multiple_of(value, 16)


def cols128(start, size):
    return pl.ds(pl.multiple_of(start, 128), size)


class Place:
    def __init__(self):
        dp = lax.axis_index("dp")
        self.i, self.j = lax.axis_index("mp"), lax.axis_index("grid")
        self.xh, self.y, self.z = lax.rem(dp, 2), lax.rem(lax.div(dp, 2), 4), lax.div(dp, 8)
        self.sib = {"grid": 1 - self.j}
        self.xa = {"mp": 1 - self.i}
        self.xb = {"dp": dp + 1 - 2 * self.xh, "mp": 1 - self.i}
        steps = (
            [2 * (lax.rem(self.y + d, 4) - self.y) for d in range(4)],
            [8 * (lax.rem(self.z + d, 4) - self.z) for d in range(4)],
        )
        flip = [0, 1 - 2 * self.xh]
        self.ring = [[{"dp": dp + r[d]} for d in (1, 2, 3)] for r in steps]
        self.eight = [[{"dp": dp + r[k // 2] + flip[k % 2]} for k in range(8)] for r in steps]

    def all(self):
        return [self.sib, self.xa, self.xb] + self.eight[0][1:] + self.eight[1][2:]


class Copies:
    def __init__(self, send, recv):
        self.send, self.recv, self.made = send, recv, {}

    def put(self, name, src, dst, device):
        at = len(self.made)
        copy = pltpu.make_async_remote_copy(
            src_ref=src, dst_ref=dst, send_sem=self.send.at[at], recv_sem=self.recv.at[at],
            device_id=device, device_id_type=MESH)
        copy.start()
        self.made[name] = copy

    def got(self, name):
        self.made[name].wait_recv()

    def finish(self):
        for copy in self.made.values():
            copy.wait_send()


class Reduce:
    def __init__(self, tag, net, at, src, out, r1, p1, r2):
        self.tag, self.net, self.at = tag, net, at
        self.src, self.out, self.r1, self.p1, self.r2 = src, out, r1, p1, r2
        self.half = src.shape[0] // 2
        self.big, self.small = self.half // 4, self.half // 32
        self.pos = ((at.y, at.z), (at.z, at.y))
        self.rings = ((at.ring[0],), (at.ring[1],))
        self.eights = (at.eight[1], at.eight[0])

    def start(self, s):
        for d in (1, 2, 3):
            to = lax.rem(self.pos[s][0] + d, 4)
            self.net.put((self.tag, 1, s, d), self.src.at[pl.ds(up16(s * self.half + to * self.big), self.big)],
                         self.r1.at[s, d - 1], self.rings[s][0][d - 1])

    def part(self, s, k):
        across = self.at.xh + (k % 2) * (1 - 2 * self.at.xh)
        return (2 * lax.rem(self.pos[s][1] + k // 2, 4) + across) * self.small

    def second(self, s):
        base = s * self.half + self.pos[s][0] * self.big
        for d in (1, 2, 3):
            self.net.got((self.tag, 1, s, d))
        for k in (1, 2, 3, 4, 5, 6, 7, 0):
            off = self.part(s, k)
            rows = pl.ds(up16(off), self.small)
            total = self.src[pl.ds(up16(base + off), self.small), :].astype(F32)
            for e in range(3):
                total = total + self.r1[s, e, rows, :].astype(F32)
            self.p1[s, rows, :] = total.astype(BF16)
            if k:
                self.net.put((self.tag, 2, s, k), self.p1.at[s, rows], self.r2.at[s, k - 1], self.eights[s][k])

    def place(self, s):
        return pl.ds(up16(s * self.half + self.pos[s][0] * self.big + self.part(s, 0)), self.small)

    def own(self, s):
        for k in range(1, 8):
            self.net.got((self.tag, 2, s, k))
        total = self.p1[s, pl.ds(up16(self.part(s, 0)), self.small), :].astype(F32)
        for e in range(7):
            total = total + self.r2[s, e].astype(F32)
        rows = self.place(s)
        self.out[rows, :] = total.astype(BF16)
        for k in range(1, 8):
            self.net.put((self.tag, 3, s, k), self.out.at[rows], self.out.at[rows], self.eights[s][k])

    def spread(self, s):
        rows = pl.ds(up16(s * self.half + self.pos[s][0] * self.big), self.big)
        for k in range(1, 8):
            self.net.got((self.tag, 3, s, k))
        for d in (1, 2, 3):
            self.net.put((self.tag, 4, s, d), self.out.at[rows], self.out.at[rows], self.rings[s][0][d - 1])

    def end(self):
        for s in (0, 1):
            for d in (1, 2, 3):
                self.net.got((self.tag, 4, s, d))


def column_sum8(values):
    return jnp.sum(values.reshape(values.shape[0] // 8, 8, values.shape[1]), axis=0)


S_QB, S_VB, S_OB, S_G1, S_H1, S_G2, S_H2, S_UB, S_DB, S_ROWS = 0, 2, 4, 10, 16, 22, 28, 34, 46, 64
V_OB, V_G1, V_H1, V_G2, V_H2, V_UB, V_DB = range(7)


def layer_kernel(
    length_ref, tokens, cotangent, qkv_ref, out_ref, up_ref, down_ref, qvb_in, ob_in, g1_in, h1_in, g2_in, h2_in,
    ub_in, db_in,
    lo_ref, ig_ref, om_ref, oa_ref, ob_ref,
    x_all, cot, normed1, n1, scale1, wown, qkvt, attt, probs, out_all, up_oth, down_oth,
    h1, n2, scale2, normed2, n2t, cott, hid, gpre, gn, gn_sib, mo, mo_sib, gh1, gb, acc, small, gattt, gt,
    g1_own, g1_sib, g1_sum, g1_far, gn1_keep, gn1_out, gn1_in, gn1_mine, gn1_far,
    gm, ga, m1, mp1, m2, a1, ap1, a2, vec, vec_up, send, recv,
):
    at = Place()
    i, j = at.i, at.j
    bar = pltpu.get_barrier_semaphore()
    peers = at.all()
    for peer in peers:
        pl.semaphore_signal(bar, inc=1, device_id=peer, device_id_type=MESH)
    pl.semaphore_wait(bar, len(peers))
    net = Copies(send, recv)
    mine, theirs = pl.ds(up16(256 * j), 256), pl.ds(up16(256 * (1 - j)), 256)
    ipart, opart = cols128(384 * i, 384), cols128(384 * (1 - i), 384)
    ihalf = pl.ds(up16(384 * i), 384)

    net.put("tok", tokens, x_all.at[mine], at.sib)
    net.put("cot", cotangent, cot.at[mine], at.sib)
    odd_y, odd_z = lax.rem(at.y, 2), lax.rem(at.z, 2)
    quarter = 2 * odd_y + odd_z
    across = (quarter + 2 - 4 * odd_y, quarter + 1 - 2 * odd_z)
    weights = (("up", up_ref, up_oth), ("down", down_ref, down_oth))

    def weight_rows(q, start, size):
        return pl.ds(up16(96 * q + start), size)

    for name, src, dst in weights:
        for n, peer in enumerate((at.xa, at.xb)):
            rows = weight_rows(quarter, 48 * n, 48)
            net.put((name, "x", n), src.at[rows], dst.at[rows], peer)
    for n, peer in enumerate((at.xa, at.xb)):
        part = 192 * j + 96 * n
        net.put(("out", n), out_ref.at[pl.ds(up16(part), 96)], out_all.at[pl.ds(up16(384 * i + part), 96)], peer)

    def pass_on(which):
        name, _, dst = weights[which]
        for n in range(2):
            net.got((name, "x", n))
        for axis in range(2):
            for n in range(2):
                rows = weight_rows(quarter, 48 * n, 48)
                net.put((name, axis, n), dst.at[rows], dst.at[rows], at.ring[axis][2 * n])

    def pass_further(which):
        name, _, dst = weights[which]
        for axis in range(2):
            net.got((name, 1 - axis, axis))
            for n in range(2):
                rows = weight_rows(across[1 - axis], 48 * axis + 32 * n, 32 - 16 * n)
                net.put((name, "d", axis, n), dst.at[rows], dst.at[rows], at.ring[axis][2 * n])

    def weight_here(which):
        name = weights[which][0]
        for axis in range(2):
            net.got((name, axis, axis))
            for n in range(2):
                net.got((name, "d", axis, n))

    x_all[mine, :] = tokens[...]
    cot[mine, :] = cotangent[...]
    out_all[ihalf, :] = out_ref[...]
    for t in range(3):
        wown[pl.ds(192 * t, 192), :] = qkv_ref[t, pl.ds(up16(192 * j), 192), :]

    def first_norm(start):
        @pl.loop(0, 4)
        def _(b):
            rows = pl.ds(up16(start + 64 * b), 64)
            v = x_all[rows, :].astype(F32)
            c = v - jnp.mean(v, axis=-1, keepdims=True)
            sc = lax.rsqrt(jnp.mean(c * c, axis=-1, keepdims=True) + EPS)
            n = c * sc
            n1[rows, :] = n
            scale1[rows, :] = jnp.broadcast_to(sc, (64, 128))
            normed1[rows, :] = (n * vec[V_G1 : V_G1 + 1, :] + vec[V_H1 : V_H1 + 1, :]).astype(BF16)

    for n, ref in enumerate((ob_in, g1_in, h1_in, g2_in, h2_in)):
        vec[n : n + 1, :] = ref[...].reshape(1, 768)
    vec[V_DB : V_DB + 1, 0:384] = db_in[...].reshape(1, 384)
    vec_up[...] = ub_in[...].reshape(1, 1536)
    first_norm(256 * j)
    net.got("tok")
    first_norm(256 * (1 - j))

    ones = jnp.ones((16, 512), BF16)
    line = lax.broadcasted_iota(jnp.int32, (16, 192), 0)

    def bias_columns(n):
        b = jnp.where(j == 0, qvb_in[n : n + 1, 0:192], qvb_in[n : n + 1, 192:384])
        t1 = b.astype(BF16).astype(F32)
        t2 = (b - t1).astype(BF16).astype(F32)
        terms = jnp.where(line == 0, t1, jnp.where(line == 1, t2, jnp.where(line == 2, b - t1 - t2, 0.0)))
        return dot(terms.astype(BF16), ones, 0, 0)

    for t in range(3):
        r = dot(wown[192 * t : 192 * t + 192, :], normed1[...], 1, 1)
        if t == 0:
            r = (r + bias_columns(0)).astype(BF16).astype(F32) * (HD**-0.5)
        if t == 2:
            r = r + bias_columns(1)
        qkvt[192 * t : 192 * t + 192, :] = r.astype(BF16)

    pass_on(0)
    length = length_ref[0]
    own_rows = 384 * i + 192 * j
    for h in range(3):
        for qb in range(2):
            kr = 256 * (qb + 1)
            qc = slice(256 * qb, 256 * qb + 256)
            kt = qkvt[192 + 64 * h : 256 + 64 * h, 0:kr]
            s = dot(kt, qkvt[64 * h : 64 * h + 64, qc], 0, 0)
            kp = lax.broadcasted_iota(jnp.int32, (kr, 256), 0)
            qp = lax.broadcasted_iota(jnp.int32, (kr, 256), 1) + 256 * qb
            s = jnp.where((kp == qp) | ((kp < qp) & (qp < length)), s, NEG)
            e = jnp.exp(s - jnp.max(s, axis=0, keepdims=True))
            p = e * (1.0 / jnp.sum(e, axis=0, keepdims=True))
            probs[h, 0:kr, qc] = p
            o = dot(qkvt[384 + 64 * h : 448 + 64 * h, 0:kr], p.astype(BF16), 1, 0)
            attt[pl.ds(up16(own_rows + 64 * h), 64), qc] = o.astype(BF16)
        rows = pl.ds(up16(own_rows + 64 * h), 64)
        for n, peer in enumerate((at.xa, at.sib)):
            net.put(("att", h, n), attt.at[rows], attt.at[rows], peer)

    pass_on(1)

    net.got("cot")
    cott[...] = cot[:, ipart].T
    small[...] = jnp.zeros_like(small)

    def put_small(row, value):
        for c in range(value.shape[1] // 128):
            small[row + c : row + c + 1, :] = value[:, 128 * c : 128 * c + 128]

    put_small(S_DB, jnp.sum(cot[:, ipart].astype(F32), axis=0, keepdims=True))
    far_rows = 384 * (1 - i) + 192 * j
    pass_further(0)
    for n in range(2):
        net.got(("out", n))
    rows = pl.ds(up16(far_rows), 192)
    net.put("outs", out_all.at[rows], out_all.at[rows], at.sib)
    pass_further(1)
    for h in range(3):
        net.got(("att", h, 0))
        rows = pl.ds(up16(far_rows + 64 * h), 64)
        net.put(("att", h, 2), attt.at[rows], attt.at[rows], at.sib)
    net.got("outs")
    for h in range(3):
        for n in (1, 2):
            net.got(("att", h, n))

    @pl.loop(0, 4)
    def _(b):
        rows = pl.ds(up16(128 * b), 128)
        v = x_all[rows, :].astype(F32) + dot(attt[:, cols128(128 * b, 128)], out_all[...], 0, 0)
        v = v + vec[V_OB : V_OB + 1, :]
        h1[rows, :] = v
        c = v - jnp.mean(v, axis=-1, keepdims=True)
        sc = lax.rsqrt(jnp.mean(c * c, axis=-1, keepdims=True) + EPS)
        n = c * sc
        n2[rows, :] = n
        scale2[rows, :] = jnp.broadcast_to(sc, (128, 128))
        normed2[rows, :] = (n * vec[V_G2 : V_G2 + 1, :] + vec[V_H2 : V_H2 + 1, :]).astype(BF16)

    n2t[...] = normed2[:, ipart].T
    weight_here(0)
    weight_here(1)

    @pl.loop(0, 6)
    def _(c):
        cs = cols128(256 * c, 256)
        pre = dot(normed2[:, ipart], up_ref[:, cs], 1, 0) + dot(normed2[:, opart], up_oth[:, cs], 1, 0)
        pre = pre + vec_up[:, cs]
        g = dot(cot[:, ipart], down_ref[:, cs], 1, 0) + dot(cot[:, opart], down_oth[:, cs], 1, 0)
        k = 0.7978845608028654
        sq = pre * pre
        t = jnp.tanh(pre * (k + (k * 0.044715) * sq))
        half = 0.5 + 0.5 * t
        hid[:, cs] = (pre * half).astype(BF16)
        slope = half + (pre * half) * (1.0 - t) * (k + (3 * 0.044715 * k) * sq)
        gp = (g * slope).astype(BF16)
        gpre[:, cs] = gp
        ub = jnp.sum(gp.astype(F32), axis=0, keepdims=True)
        acc[24:25, cs] = ub

    for c in range(2):
        rows = pl.ds(256 * c, 256)
        gn[rows, ipart] = dot(gpre[rows, :], up_ref[...], 1, 1).astype(BF16)
        gn[rows, opart] = dot(gpre[rows, :], up_oth[...], 1, 1).astype(BF16)
        net.put(("gn", c), gn.at[rows], gn_sib.at[rows], at.sib)

    big = Reduce("m", net, at, gm, om_ref, m1, mp1, m2)
    for s, left, right in ((1, cott, hid), (0, n2t, gpre)):
        @pl.loop(0, 6)
        def _(c):
            r = dot(left[...], right[:, cols128(256 * c, 256)], 1, 0).astype(BF16)
            for b in range(2):
                gm[pl.ds(up16(4608 * s + 384 * (2 * c + b)), 384), :] = r[:, 128 * b : 128 * b + 128]
        big.start(s)

    mo[...] = dot(hid[theirs, :], down_ref[...], 1, 1)
    net.put("mo", mo, mo_sib, at.sib)
    lo_part = dot(hid[mine, :], down_ref[...], 1, 1) + h1[mine, ipart] + vec[V_DB : V_DB + 1, 0:384]

    acc[0:24, 0:768] = jnp.zeros((24, 768), F32)
    for c in range(2):
        net.got(("gn", c))

    @pl.loop(0, 8)
    def _(b):
        rows = pl.ds(up16(64 * b), 64)
        g = gn[rows, :].astype(F32) + gn_sib[rows, :].astype(F32)
        n = n2[rows, :]
        e = g * vec[V_G2 : V_G2 + 1, :]
        m = jnp.mean(e, axis=-1, keepdims=True)
        mn = jnp.mean(e * n, axis=-1, keepdims=True)
        v = cot[rows, :].astype(F32) + (e - m - n * mn) * scale2[rows, 0:1]
        gh1[rows, :] = v
        low = v.astype(BF16)
        gb[rows, :] = low
        acc[0:8, 0:768] += column_sum8(g * n)
        acc[8:16, 0:768] += column_sum8(g)
        acc[16:24, 0:768] += column_sum8(low.astype(F32))

    put_small(S_G2, jnp.sum(acc[0:8, 0:768], axis=0, keepdims=True))
    put_small(S_H2, jnp.sum(acc[8:16, 0:768], axis=0, keepdims=True))
    put_small(S_OB, jnp.sum(acc[16:24, 0:768], axis=0, keepdims=True))
    put_small(S_UB, acc[24:25, :])

    gattt[...] = dot(out_ref[pl.ds(up16(192 * j), 192), :], gb[...], 1, 1).astype(BF16)
    net.got("mo")
    lo_ref[...] = (lo_part + mo_sib[...]).astype(BF16)

    for h in range(3):
        hs = slice(64 * h, 64 * h + 64)
        gk, gv = [], []
        for qb in range(2):
            kr = 256 * (qb + 1)
            qc = slice(256 * qb, 256 * qb + 256)
            p = probs[h, 0:kr, qc]
            gat = gattt[hs, qc]
            g = dot(qkvt[384 + 64 * h : 448 + 64 * h, 0:kr], gat, 0, 0)
            delta = jnp.sum(p * g, axis=0, keepdims=True)
            gs = (p * (g - delta)).astype(BF16)
            gt[hs, qc] = (dot(qkvt[192 + 64 * h : 256 + 64 * h, 0:kr], gs, 1, 0) * (HD**-0.5)).astype(BF16)
            gk.append(dot(qkvt[hs, qc], gs, 1, 1))
            gv.append(dot(gat, p.astype(BF16), 1, 1))
        for base, parts in ((192, gk), (384, gv)):
            rows = slice(base + 64 * h, base + 64 * h + 64)
            gt[rows, 0:256] = (parts[0] + parts[1][:, 0:256]).astype(BF16)
            gt[rows, 256:512] = parts[1][:, 256:512].astype(BF16)

    @pl.loop(0, 2)
    def _(b):
        rows = pl.ds(up16(128 * b), 128)
        r = dot(gt[:, cols128(256 * (1 - j) + 128 * b, 128)], wown[...], 0, 0)
        gn1_out[rows, :] = r.astype(BF16)
        gn1_keep[pl.ds(up16(256 * (1 - j) + 128 * b), 128), :] = r

    net.put("gn1", gn1_out, gn1_in, at.sib)

    @pl.loop(0, 2)
    def _(b):
        r = dot(gt[:, cols128(256 * j + 128 * b, 128)], wown[...], 0, 0)
        gn1_keep[pl.ds(up16(256 * j + 128 * b), 128), :] = r

    acc[0:16, 0:768] = jnp.zeros((16, 768), F32)

    @pl.loop(0, 8)
    def _(b):
        rows = pl.ds(up16(64 * b), 64)
        g = gn1_keep[rows, :]
        acc[0:8, 0:768] += column_sum8(g * n1[rows, :])
        acc[8:16, 0:768] += column_sum8(g)

    for n in range(2):
        g1_own[8 * n : 8 * n + 8, :] = jnp.broadcast_to(
            jnp.sum(acc[8 * n : 8 * n + 8, 0:768], axis=0, keepdims=True), (8, 768))
    net.put("g1", g1_own, g1_sib, at.sib)
    for base, row in ((0, S_QB), (384, S_VB)):
        r = dot(ones, gt[base : base + 192, :], 1, 1)
        small[row : row + 1, :] = r[0:1, 0:128]
        small[row + 1 : row + 2, 0:64] = r[0:1, 128:192]
    net.got("g1")
    g1_sum[...] = g1_own[...] + g1_sib[...]
    net.put("g1x", g1_sum, g1_far, at.xa)
    net.got("gn1")
    half_sum = gn1_keep[mine, :] + gn1_in[...].astype(F32)
    gn1_mine[...] = half_sum.astype(BF16)
    for n in range(3):
        r = dot(gt[192 * n : 192 * n + 192, :], normed1[...], 1, 0).astype(BF16)
        for c in range(6):
            ga[pl.ds(576 * c + 192 * n, 192), :] = r[:, 128 * c : 128 * c + 128]
    r = dot(attt[pl.ds(up16(own_rows), 192), :], gb[...], 1, 0).astype(BF16)
    for c in range(6):
        ga[pl.ds(3456 + 192 * c, 192), :] = r[:, 128 * c : 128 * c + 128]
    ga[pl.ds(4608 + S_ROWS, 512 - S_ROWS), :] = jnp.zeros((512 - S_ROWS, 128), BF16)
    tail = Reduce("a", net, at, ga, oa_ref, a1, ap1, a2)
    tail.start(0)

    net.got("g1x")
    g1_own_sum = g1_sum[...] + g1_far[...]
    put_small(S_G1, g1_own_sum[0:1, :])
    put_small(S_H1, g1_own_sum[8:9, :])
    ga[pl.ds(4608, S_ROWS), :] = small[...].astype(BF16)
    tail.start(1)
    big.second(1)
    big.second(0)
    tail.second(0)
    tail.second(1)
    big.own(1)
    big.own(0)
    tail.own(0)
    tail.own(1)
    net.put("gn1x", gn1_mine, gn1_far, at.xa)
    big.spread(1)
    big.spread(0)
    tail.spread(0)
    tail.spread(1)
    net.got("gn1x")

    @pl.loop(0, 4)
    def _(b):
        rows = pl.ds(up16(64 * b), 64)
        full = pl.ds(up16(256 * j + 64 * b), 64)
        g = gn1_mine[rows, :].astype(F32) + gn1_far[rows, :].astype(F32)
        n = n1[full, :]
        e = g * vec[V_G1 : V_G1 + 1, :]
        m = jnp.mean(e, axis=-1, keepdims=True)
        mn = jnp.mean(e * n, axis=-1, keepdims=True)
        ig_ref[rows, :] = gh1[full, :] + (e - m - n * mn) * scale1[full, 0:1]

    big.end()
    tail.end()
    net.put("sib", oa_ref, ob_ref, at.sib)
    net.got("sib")
    net.finish()


def layer_call(*args):
    V = pltpu.VMEM
    sds = jax.ShapeDtypeStruct
    scratch = [
        V((512, 768), BF16), V((512, 768), BF16), V((512, 768), BF16), V((512, 768), F32), V((512, 128), F32),
        V((576, 768), BF16), V((576, 512), BF16), V((768, 512), BF16), V((3, 512, 512), F32), V((768, 768), BF16),
        V((384, 1536), BF16), V((384, 1536), BF16),
        V((512, 768), F32), V((512, 768), F32), V((512, 128), F32), V((512, 768), BF16), V((384, 512), BF16),
        V((384, 512), BF16), V((512, 1536), BF16), V((512, 1536), BF16), V((512, 768), BF16), V((512, 768), BF16),
        V((256, 384), F32), V((256, 384), F32), V((512, 768), F32), V((512, 768), BF16), V((32, 1536), F32),
        V((S_ROWS, 128), F32), V((192, 512), BF16), V((576, 512), BF16),
        V((16, 768), F32), V((16, 768), F32), V((16, 768), F32), V((16, 768), F32),
        V((512, 768), F32), V((256, 768), BF16), V((256, 768), BF16), V((256, 768), BF16), V((256, 768), BF16),
        V((9216, 128), BF16), V((5120, 128), BF16),
        V((2, 3, 1152, 128), BF16), V((2, 1152, 128), BF16), V((2, 7, 144, 128), BF16),
        V((2, 3, 640, 128), BF16), V((2, 640, 128), BF16), V((2, 7, 80, 128), BF16),
        V((8, 768), F32), V((1, 1536), F32),
        pltpu.SemaphoreType.DMA((160,)), pltpu.SemaphoreType.DMA((160,)),
    ]
    vm = pl.BlockSpec(memory_space=V)
    return pl.pallas_call(
        layer_kernel,
        out_shape=(sds((256, 384), BF16), sds((256, 768), F32), sds((9216, 128), BF16), sds((5120, 128), BF16),
                   sds((5120, 128), BF16)),
        in_specs=[pl.BlockSpec(memory_space=pltpu.SMEM)] + [vm] * 14,
        out_specs=(vm,) * 5,
        scratch_shapes=scratch,
        compiler_params=pltpu.CompilerParams(collective_id=0, has_side_effects=True, vmem_limit_bytes=60 << 20),
        name="layer",
    )(*args)


def finish_kernel(lo, ig, om_in, oa_in, ob_in, lo_out, ig_out, qkv_out, qvb_out, ow_out, out_bias, gain1, shift1, gain2, shift2,
                  up_out, up_bias, down_out, down_bias, qkv, ow, up, down, om, oa, ob,
                  sems, in_sems):
    j = lax.axis_index("grid")
    copies = []
    halves = [pl.ds(4608 * s, 4608) for s in range(2)]
    fetch = [
        pltpu.make_async_copy(src, dst, in_sems.at[n])
        for n, (src, dst) in enumerate(
            [(om_in.at[h], om.at[h]) for h in halves] + [(oa_in, oa), (ob_in, ob)])
    ]
    for copy in fetch:
        copy.start()

    def send(src, dst):
        copy = pltpu.make_async_copy(src, dst, sems.at[len(copies)])
        copy.start()
        copies.append(copy)

    send(lo, lo_out)
    send(ig, ig_out)
    for s, scr, dst in ((0, up, up_out), (1, down, down_out)):
        fetch[s].wait()
        for c in range(12):
            scr[:, 128 * c : 128 * c + 128] = om[4608 * s + 384 * c : 4608 * s + 384 * c + 384, :].astype(F32)
        send(scr, dst)
    fetch[2].wait()
    fetch[3].wait()
    for src, side in ((oa, j), (ob, 1 - j)):
        rows = pl.ds(pl.multiple_of(192 * side, 192), 192)
        for c in range(6):
            ow[rows, 128 * c : 128 * c + 128] = src[3456 + 192 * c : 3648 + 192 * c, :].astype(F32)
    send(ow, ow_out)
    for n in range(3):
        for src, side in ((oa, j), (ob, 1 - j)):
            rows = pl.ds(pl.multiple_of(192 * side, 192), 192)
            for c in range(6):
                at = 576 * c + 192 * n
                qkv[n, rows, 128 * c : 128 * c + 128] = src[at : at + 192, :].astype(F32)
        send(qkv.at[n], qkv_out.at[n])
    mine, other = (a[4608 : 4608 + S_ROWS, :].astype(F32) for a in (oa, ob))
    first, second = jnp.where(j == 0, mine, other), jnp.where(j == 0, other, mine)
    for n in range(2):
        qvb_out[n : n + 1, :] = jnp.concatenate(
            [part[2 * n + c : 2 * n + c + 1, : 128 - 64 * c] for part in (first, second) for c in range(2)], axis=1)
    for dst, row, count in ((out_bias, S_OB, 6), (gain1, S_G1, 6), (shift1, S_H1, 6), (gain2, S_G2, 6),
                            (shift2, S_H2, 6), (up_bias, S_UB, 12), (down_bias, S_DB, 3)):
        for c in range(count):
            dst[128 * c : 128 * c + 128] = mine[row + c]
    for copy in copies:
        copy.wait()


def finish(*args):
    V, hbm = pl.BlockSpec(memory_space=pltpu.VMEM), pl.BlockSpec(memory_space=pltpu.HBM)
    f = lambda *shape: jax.ShapeDtypeStruct(shape, F32)
    return pl.pallas_call(
        finish_kernel,
        out_shape=(jax.ShapeDtypeStruct((256, 384), BF16), f(256, 768), f(3, 384, 768), f(2, 384), f(384, 768),
                   f(768), f(768), f(768), f(768), f(768), f(384, 1536), f(1536), f(384, 1536), f(384)),
        in_specs=[hbm] * 5,
        out_specs=(hbm, hbm, hbm, V, hbm, V, V, V, V, V, hbm, V, hbm, V),
        scratch_shapes=[pltpu.VMEM((3, 384, 768), F32), pltpu.VMEM((384, 768), F32), pltpu.VMEM((384, 1536), F32),
                        pltpu.VMEM((384, 1536), F32), pltpu.VMEM((9216, 128), BF16), pltpu.VMEM((5120, 128), BF16),
                        pltpu.VMEM((5120, 128), BF16), pltpu.SemaphoreType.DMA((8,)), pltpu.SemaphoreType.DMA((4,))],
        compiler_params=pltpu.CompilerParams(vmem_limit_bytes=40 << 20),
        name="finish",
    )(*args)


def per_device(tokens, seq_lengths, cotangent, qkv_weight, qv_bias, out_weight, out_bias,
               first_gain, first_shift, second_gain, second_shift, up_weight, up_bias, down_weight, down_bias):
    return finish(*layer_call(
        seq_lengths, tokens, cotangent, qkv_weight, out_weight, up_weight, down_weight, qv_bias, out_bias,
        first_gain, first_shift, second_gain, second_shift, up_bias, down_bias))


def solution(mesh):
    placed = (
        P(("dp", "grid"), None), P("dp"), P(("dp", "grid"), None), P(None, "mp", None), P(None, "mp"),
        P("mp", None), P(), P(), P(), P(), P(), P("mp", "grid"), P("grid"), P("mp", "grid"), P("mp"),
    )
    return jax.shard_map(
        per_device,
        mesh=mesh,
        in_specs=placed,
        out_specs=(
            P(("dp", "grid"), "mp"), P(("dp", "grid"), None), P(None, "mp", None), P(None, "mp"), P("mp", None),
            P(), P(), P(), P(), P(), P("mp", "grid"), P("grid"), P("mp", "grid"), P("mp"),
        ),
        check_vma=False,
    )
```

```python
import functools

import jax
import jax.numpy as jnp
from jax import lax
from jax.experimental import pallas as pl
from jax.experimental.pallas import tpu as pltpu
from jax.sharding import PartitionSpec as P

HD = 64
EPS = 1e-05
NEG = -1e30
MESH = pl.DeviceIdType.MESH
F32, BF16 = jnp.float32, jnp.bfloat16


def dot(left, right, left_dim, right_dim):
    return lax.dot_general(
        left, right, (((left_dim,), (right_dim,)), ((), ())), preferred_element_type=F32
    )


def up16(value):
    return pl.multiple_of(value, 16)


def cols128(start, size):
    return pl.ds(pl.multiple_of(start, 128), size)


class Place:
    def __init__(self):
        dp = lax.axis_index("dp")
        self.i, self.j = lax.axis_index("mp"), lax.axis_index("grid")
        self.xh, self.y, self.z = lax.rem(dp, 2), lax.rem(lax.div(dp, 2), 4), lax.div(dp, 8)
        self.sib = {"grid": 1 - self.j}
        self.xa = {"mp": 1 - self.i}
        self.xb = {"dp": dp + 1 - 2 * self.xh, "mp": 1 - self.i}
        steps = (
            [2 * (lax.rem(self.y + d, 4) - self.y) for d in range(4)],
            [8 * (lax.rem(self.z + d, 4) - self.z) for d in range(4)],
        )
        flip = [0, 1 - 2 * self.xh]
        self.ring = [[{"dp": dp + r[d]} for d in (1, 2, 3)] for r in steps]
        self.eight = [[{"dp": dp + r[k // 2] + flip[k % 2]} for k in range(8)] for r in steps]

    def all(self):
        return [self.sib, self.xa, self.xb] + self.eight[0][1:] + self.eight[1][2:]


class Copies:
    def __init__(self, send, recv):
        self.send, self.recv, self.made = send, recv, {}

    def put(self, name, src, dst, device):
        at = len(self.made)
        copy = pltpu.make_async_remote_copy(
            src_ref=src, dst_ref=dst, send_sem=self.send.at[at], recv_sem=self.recv.at[at],
            device_id=device, device_id_type=MESH)
        copy.start()
        self.made[name] = copy

    def got(self, name):
        self.made[name].wait_recv()

    def finish(self):
        for copy in self.made.values():
            copy.wait_send()


class Reduce:
    def __init__(self, tag, net, at, src, out, r1, p1, r2, twin=None):
        self.tag, self.net, self.at, self.twin = tag, net, at, twin
        self.src, self.out, self.r1, self.p1, self.r2 = src, out, r1, p1, r2
        self.half = src.shape[0] // 2
        self.big, self.small = self.half // 4, self.half // 32
        self.pos = ((at.y, at.z), (at.z, at.y))
        self.rings = ((at.ring[0],), (at.ring[1],))
        self.eights = (at.eight[1], at.eight[0])

    def start(self, s):
        for d in (1, 2, 3):
            to = lax.rem(self.pos[s][0] + d, 4)
            self.net.put((self.tag, 1, s, d), self.src.at[pl.ds(up16(s * self.half + to * self.big), self.big)],
                         self.r1.at[s, d - 1], self.rings[s][0][d - 1])

    def part(self, s, k):
        across = self.at.xh + (k % 2) * (1 - 2 * self.at.xh)
        return (2 * lax.rem(self.pos[s][1] + k // 2, 4) + across) * self.small

    def second(self, s):
        base = s * self.half + self.pos[s][0] * self.big
        for d in (1, 2, 3):
            self.net.got((self.tag, 1, s, d))
        for k in (1, 2, 3, 4, 5, 6, 7, 0):
            off = self.part(s, k)
            rows = pl.ds(up16(off), self.small)
            total = self.src[pl.ds(up16(base + off), self.small), :].astype(F32)
            for e in range(3):
                total = total + self.r1[s, e, rows, :].astype(F32)
            self.p1[s, rows, :] = total.astype(BF16)
            if k:
                self.net.put((self.tag, 2, s, k), self.p1.at[s, rows], self.r2.at[s, k - 1], self.eights[s][k])

    def place(self, s):
        return pl.ds(up16(s * self.half + self.pos[s][0] * self.big + self.part(s, 0)), self.small)

    def own(self, s):
        for k in range(1, 8):
            self.net.got((self.tag, 2, s, k))
        total = self.p1[s, pl.ds(up16(self.part(s, 0)), self.small), :].astype(F32)
        for e in range(7):
            total = total + self.r2[s, e].astype(F32)
        rows = self.place(s)
        self.out[rows, :] = total.astype(BF16)
        for k in range(1, 8):
            self.net.put((self.tag, 3, s, k), self.out.at[rows], self.out.at[rows], self.eights[s][k])

    def piece(self, s, d, start, size):
        to = lax.rem(self.pos[s][0] + d, 4)
        return pl.ds(up16(s * self.half + to * self.big + start), size)

    def give(self, name, rows, device):
        self.net.put((self.tag,) + name, self.out.at[rows], self.out.at[rows], device)

    def mirror(self, s, d):
        if self.twin is not None:
            rows = self.piece(s, d, 0, self.big)
            self.net.put((self.tag, 6, s, d), self.out.at[rows], self.twin.at[rows], self.at.sib)

    def spread(self, s):
        for k in range(1, 8):
            self.net.got((self.tag, 3, s, k))
        for d in (1, 3):
            self.give((4, s, d), self.piece(s, 0, 0, self.big), self.rings[s][0][d - 1])
        self.mirror(s, 0)

    def relay(self, s):
        h = self.big // 2
        for d, start in ((1, 0), (3, h)):
            self.net.got((self.tag, 4, s, d))
            self.give((5, s, d), self.piece(s, 4 - d, start, h), self.rings[s][0][d - 1])
        for d in (1, 3):
            self.mirror(s, d)

    def end(self, s):
        for d in (1, 3):
            self.net.got((self.tag, 5, s, d))
        self.mirror(s, 2)

    def mirrored(self):
        for s in (0, 1):
            for d in range(4):
                self.net.got((self.tag, 6, s, d))


def column_sum8(values):
    return jnp.sum(values.reshape(values.shape[0] // 8, 8, values.shape[1]), axis=0)


S_QB, S_VB, S_OB, S_G1, S_H1, S_G2, S_H2, S_UB, S_DB, S_ROWS = 0, 2, 4, 10, 16, 22, 28, 34, 46, 64
V_OB, V_G1, V_H1, V_G2, V_H2, V_UB, V_DB = range(7)


def layer_kernel(
    length_ref, tokens, cotangent, qkv_in, out_in, up_in, down_in, qvb_in, ob_in, g1_in, h1_in, g2_in, h2_in,
    ub_in, db_in,
    lo_ref, ig_ref, om_ref, oa_ref, ob_ref,
    x_all, cot, normed1, n1, scale1, wown, qkvt, attt, probs, out_all, up_oth, down_oth,
    h1, n2, scale2, normed2, n2t, cott, hid, gpre, gn, gn_sib, mo, mo_sib, gh1, gb, acc, small, gattt, gt,
    g1_own, g1_sib, g1_sum, g1_far, gn1_keep, gn1_out, gn1_in, gn1_mine, gn1_far,
    gm, ga, m1, mp1, m2, a1, ap1, a2, vec, vec_up, up_ref, down_ref, send, recv, near,
):
    at = Place()
    i, j = at.i, at.j
    mine, theirs = pl.ds(up16(256 * j), 256), pl.ds(up16(256 * (1 - j)), 256)
    ihalf = pl.ds(up16(384 * i), 384)
    local = [(tokens, x_all.at[mine])]
    local += [(qkv_in.at[t, pl.ds(up16(192 * j), 192)], wown.at[pl.ds(192 * t, 192)]) for t in range(3)]
    local += [(cotangent, cot.at[mine]), (out_in, out_all.at[ihalf]), (up_in, up_ref), (down_in, down_ref)]
    local = [pltpu.make_async_copy(src, dst, near.at[n]) for n, (src, dst) in enumerate(local)]
    for copy in local:
        copy.start()
    bar = pltpu.get_barrier_semaphore()
    peers = at.all()
    for peer in peers:
        pl.semaphore_signal(bar, inc=1, device_id=peer, device_id_type=MESH)
    pl.semaphore_wait(bar, len(peers))
    net = Copies(send, recv)
    ipart, opart = cols128(384 * i, 384), cols128(384 * (1 - i), 384)

    net.put("tok", tokens, x_all.at[mine], at.sib)
    net.put("cot", cotangent, cot.at[mine], at.sib)
    odd_y, odd_z = lax.rem(at.y, 2), lax.rem(at.z, 2)
    quarter = 2 * odd_y + odd_z
    across = (quarter + 2 - 4 * odd_y, quarter + 1 - 2 * odd_z)
    weights = (("up", up_in, up_oth), ("down", down_in, down_oth))

    def weight_rows(q, start, size):
        return pl.ds(up16(96 * q + start), size)

    for name, src, dst in weights:
        for n, peer in enumerate((at.xa, at.xb)):
            rows = weight_rows(quarter, 48 * n, 48)
            net.put((name, "x", n), src.at[rows], dst.at[rows], peer)
    for n, peer in enumerate((at.xa, at.xb)):
        part = 192 * j + 96 * n
        net.put(("out", n), out_in.at[pl.ds(up16(part), 96)], out_all.at[pl.ds(up16(384 * i + part), 96)], peer)

    def pass_on(which):
        name, _, dst = weights[which]
        for n in range(2):
            net.got((name, "x", n))
        for axis in range(2):
            for n in range(2):
                rows = weight_rows(quarter, 48 * n, 48)
                net.put((name, axis, n), dst.at[rows], dst.at[rows], at.ring[axis][2 * n])

    def pass_further(which):
        name, _, dst = weights[which]
        for axis in range(2):
            net.got((name, 1 - axis, axis))
            for n in range(2):
                rows = weight_rows(across[1 - axis], 48 * axis + 32 * n, 32 - 16 * n)
                net.put((name, "d", axis, n), dst.at[rows], dst.at[rows], at.ring[axis][2 * n])

    def weight_here(which):
        name = weights[which][0]
        for axis in range(2):
            net.got((name, axis, axis))
            for n in range(2):
                net.got((name, "d", axis, n))

    def first_norm(start):
        @pl.loop(0, 4)
        def _(b):
            rows = pl.ds(up16(start + 64 * b), 64)
            v = x_all[rows, :].astype(F32)
            c = v - jnp.mean(v, axis=-1, keepdims=True)
            sc = lax.rsqrt(jnp.mean(c * c, axis=-1, keepdims=True) + EPS)
            n = c * sc
            n1[rows, :] = n
            scale1[rows, :] = jnp.broadcast_to(sc, (64, 128))
            normed1[rows, :] = (n * vec[V_G1 : V_G1 + 1, :] + vec[V_H1 : V_H1 + 1, :]).astype(BF16)

    for n, ref in enumerate((ob_in, g1_in, h1_in, g2_in, h2_in)):
        vec[n : n + 1, :] = ref[...].reshape(1, 768)
    vec[V_DB : V_DB + 1, 0:384] = db_in[...].reshape(1, 384)
    vec_up[...] = ub_in[...].reshape(1, 1536)
    local[0].wait()
    first_norm(256 * j)
    net.got("tok")
    first_norm(256 * (1 - j))
    for copy in local[1:4]:
        copy.wait()

    ones = jnp.ones((16, 512), BF16)
    line = lax.broadcasted_iota(jnp.int32, (16, 192), 0)

    def bias_columns(n):
        b = jnp.where(j == 0, qvb_in[n : n + 1, 0:192], qvb_in[n : n + 1, 192:384])
        t1 = b.astype(BF16).astype(F32)
        t2 = (b - t1).astype(BF16).astype(F32)
        terms = jnp.where(line == 0, t1, jnp.where(line == 1, t2, jnp.where(line == 2, b - t1 - t2, 0.0)))
        return dot(terms.astype(BF16), ones, 0, 0)

    for t in range(3):
        r = dot(wown[192 * t : 192 * t + 192, :], normed1[...], 1, 1)
        if t == 0:
            r = (r + bias_columns(0)).astype(BF16).astype(F32) * (HD**-0.5)
        if t == 2:
            r = r + bias_columns(1)
        qkvt[192 * t : 192 * t + 192, :] = r.astype(BF16)

    pass_on(0)
    length = length_ref[0]
    own_rows = 384 * i + 192 * j
    for h in range(3):
        for qb in range(2):
            kr = 256 * (qb + 1)
            qc = slice(256 * qb, 256 * qb + 256)
            kt = qkvt[192 + 64 * h : 256 + 64 * h, 0:kr]
            s = dot(kt, qkvt[64 * h : 64 * h + 64, qc], 0, 0)
            kp = lax.broadcasted_iota(jnp.int32, (kr, 256), 0)
            qp = lax.broadcasted_iota(jnp.int32, (kr, 256), 1) + 256 * qb
            s = jnp.where((kp == qp) | ((kp < qp) & (qp < length)), s, NEG)
            e = jnp.exp(s - jnp.max(s, axis=0, keepdims=True))
            p = e * (1.0 / jnp.sum(e, axis=0, keepdims=True))
            probs[h, 0:kr, qc] = p
            o = dot(qkvt[384 + 64 * h : 448 + 64 * h, 0:kr], p.astype(BF16), 1, 0)
            attt[pl.ds(up16(own_rows + 64 * h), 64), qc] = o.astype(BF16)
        rows = pl.ds(up16(own_rows + 64 * h), 64)
        for n, peer in enumerate((at.xa, at.sib)):
            net.put(("att", h, n), attt.at[rows], attt.at[rows], peer)

    pass_on(1)

    for copy in local[4:]:
        copy.wait()
    net.got("cot")
    cott[...] = cot[:, ipart].T
    small[...] = jnp.zeros_like(small)

    def put_small(row, value):
        for c in range(value.shape[1] // 128):
            small[row + c : row + c + 1, :] = value[:, 128 * c : 128 * c + 128]

    put_small(S_DB, jnp.sum(cot[:, ipart].astype(F32), axis=0, keepdims=True))
    far_rows = 384 * (1 - i) + 192 * j
    pass_further(0)
    for n in range(2):
        net.got(("out", n))
    rows = pl.ds(up16(far_rows), 192)
    net.put("outs", out_all.at[rows], out_all.at[rows], at.sib)
    pass_further(1)
    for h in range(3):
        net.got(("att", h, 0))
        rows = pl.ds(up16(far_rows + 64 * h), 64)
        net.put(("att", h, 2), attt.at[rows], attt.at[rows], at.sib)
    net.got("outs")
    for h in range(3):
        for n in (1, 2):
            net.got(("att", h, n))

    @pl.loop(0, 4)
    def _(b):
        rows = pl.ds(up16(128 * b), 128)
        v = x_all[rows, :].astype(F32) + dot(attt[:, cols128(128 * b, 128)], out_all[...], 0, 0)
        v = v + vec[V_OB : V_OB + 1, :]
        h1[rows, :] = v
        c = v - jnp.mean(v, axis=-1, keepdims=True)
        sc = lax.rsqrt(jnp.mean(c * c, axis=-1, keepdims=True) + EPS)
        n = c * sc
        n2[rows, :] = n
        scale2[rows, :] = jnp.broadcast_to(sc, (128, 128))
        normed2[rows, :] = (n * vec[V_G2 : V_G2 + 1, :] + vec[V_H2 : V_H2 + 1, :]).astype(BF16)

    n2t[...] = normed2[:, ipart].T
    weight_here(0)
    weight_here(1)

    @pl.loop(0, 6)
    def _(c):
        cs = cols128(256 * c, 256)
        pre = dot(normed2[:, ipart], up_ref[:, cs], 1, 0) + dot(normed2[:, opart], up_oth[:, cs], 1, 0)
        pre = pre + vec_up[:, cs]
        g = dot(cot[:, ipart], down_ref[:, cs], 1, 0) + dot(cot[:, opart], down_oth[:, cs], 1, 0)
        k = 0.7978845608028654
        sq = pre * pre
        t = jnp.tanh(pre * (k + (k * 0.044715) * sq))
        half = 0.5 + 0.5 * t
        hid[:, cs] = (pre * half).astype(BF16)
        slope = half + (pre * half) * (1.0 - t) * (k + (3 * 0.044715 * k) * sq)
        gp = (g * slope).astype(BF16)
        gpre[:, cs] = gp
        ub = jnp.sum(gp.astype(F32), axis=0, keepdims=True)
        acc[24:25, cs] = ub

    for c in range(2):
        rows = pl.ds(256 * c, 256)
        gn[rows, ipart] = dot(gpre[rows, :], up_ref[...], 1, 1).astype(BF16)
        gn[rows, opart] = dot(gpre[rows, :], up_oth[...], 1, 1).astype(BF16)
        net.put(("gn", c), gn.at[rows], gn_sib.at[rows], at.sib)

    big = Reduce("m", net, at, gm, om_ref, m1, mp1, m2)
    for s, left, right in ((1, cott, hid), (0, n2t, gpre)):
        @pl.loop(0, 6)
        def _(c):
            r = dot(left[...], right[:, cols128(256 * c, 256)], 1, 0).astype(BF16)
            for b in range(2):
                gm[pl.ds(up16(4608 * s + 384 * (2 * c + b)), 384), :] = r[:, 128 * b : 128 * b + 128]
        big.start(s)

    mo[...] = dot(hid[theirs, :], down_ref[...], 1, 1)
    net.put("mo", mo, mo_sib, at.sib)
    lo_part = dot(hid[mine, :], down_ref[...], 1, 1) + h1[mine, ipart] + vec[V_DB : V_DB + 1, 0:384]

    acc[0:24, 0:768] = jnp.zeros((24, 768), F32)
    for c in range(2):
        net.got(("gn", c))

    @pl.loop(0, 8)
    def _(b):
        rows = pl.ds(up16(64 * b), 64)
        g = gn[rows, :].astype(F32) + gn_sib[rows, :].astype(F32)
        n = n2[rows, :]
        e = g * vec[V_G2 : V_G2 + 1, :]
        m = jnp.mean(e, axis=-1, keepdims=True)
        mn = jnp.mean(e * n, axis=-1, keepdims=True)
        v = cot[rows, :].astype(F32) + (e - m - n * mn) * scale2[rows, 0:1]
        gh1[rows, :] = v
        low = v.astype(BF16)
        gb[rows, :] = low
        acc[0:8, 0:768] += column_sum8(g * n)
        acc[8:16, 0:768] += column_sum8(g)
        acc[16:24, 0:768] += column_sum8(low.astype(F32))

    put_small(S_G2, jnp.sum(acc[0:8, 0:768], axis=0, keepdims=True))
    put_small(S_H2, jnp.sum(acc[8:16, 0:768], axis=0, keepdims=True))
    put_small(S_OB, jnp.sum(acc[16:24, 0:768], axis=0, keepdims=True))
    put_small(S_UB, acc[24:25, :])

    gattt[...] = dot(out_all[pl.ds(up16(own_rows), 192), :], gb[...], 1, 1).astype(BF16)
    net.got("mo")
    lo_ref[...] = (lo_part + mo_sib[...]).astype(BF16)

    for h in range(3):
        hs = slice(64 * h, 64 * h + 64)
        gk, gv = [], []
        for qb in range(2):
            kr = 256 * (qb + 1)
            qc = slice(256 * qb, 256 * qb + 256)
            p = probs[h, 0:kr, qc]
            gat = gattt[hs, qc]
            g = dot(qkvt[384 + 64 * h : 448 + 64 * h, 0:kr], gat, 0, 0)
            delta = jnp.sum(p * g, axis=0, keepdims=True)
            gs = (p * (g - delta)).astype(BF16)
            gt[hs, qc] = (dot(qkvt[192 + 64 * h : 256 + 64 * h, 0:kr], gs, 1, 0) * (HD**-0.5)).astype(BF16)
            gk.append(dot(qkvt[hs, qc], gs, 1, 1))
            gv.append(dot(gat, p.astype(BF16), 1, 1))
        for base, parts in ((192, gk), (384, gv)):
            rows = slice(base + 64 * h, base + 64 * h + 64)
            gt[rows, 0:256] = (parts[0] + parts[1][:, 0:256]).astype(BF16)
            gt[rows, 256:512] = parts[1][:, 256:512].astype(BF16)

    @pl.loop(0, 2)
    def _(b):
        rows = pl.ds(up16(128 * b), 128)
        r = dot(gt[:, cols128(256 * (1 - j) + 128 * b, 128)], wown[...], 0, 0)
        gn1_out[rows, :] = r.astype(BF16)
        gn1_keep[pl.ds(up16(256 * (1 - j) + 128 * b), 128), :] = r

    net.put("gn1", gn1_out, gn1_in, at.sib)

    @pl.loop(0, 2)
    def _(b):
        r = dot(gt[:, cols128(256 * j + 128 * b, 128)], wown[...], 0, 0)
        gn1_keep[pl.ds(up16(256 * j + 128 * b), 128), :] = r

    acc[0:16, 0:768] = jnp.zeros((16, 768), F32)

    @pl.loop(0, 8)
    def _(b):
        rows = pl.ds(up16(64 * b), 64)
        g = gn1_keep[rows, :]
        acc[0:8, 0:768] += column_sum8(g * n1[rows, :])
        acc[8:16, 0:768] += column_sum8(g)

    for n in range(2):
        g1_own[8 * n : 8 * n + 8, :] = jnp.broadcast_to(
            jnp.sum(acc[8 * n : 8 * n + 8, 0:768], axis=0, keepdims=True), (8, 768))
    net.put("g1", g1_own, g1_sib, at.sib)
    for base, row in ((0, S_QB), (384, S_VB)):
        r = dot(ones, gt[base : base + 192, :], 1, 1)
        small[row : row + 1, :] = r[0:1, 0:128]
        small[row + 1 : row + 2, 0:64] = r[0:1, 128:192]
    net.got("g1")
    g1_sum[...] = g1_own[...] + g1_sib[...]
    net.put("g1x", g1_sum, g1_far, at.xa)
    net.got("gn1")
    half_sum = gn1_keep[mine, :] + gn1_in[...].astype(F32)
    gn1_mine[...] = half_sum.astype(BF16)
    for n in range(3):
        r = dot(gt[192 * n : 192 * n + 192, :], normed1[...], 1, 0).astype(BF16)
        for c in range(6):
            ga[pl.ds(576 * c + 192 * n, 192), :] = r[:, 128 * c : 128 * c + 128]
    r = dot(attt[pl.ds(up16(own_rows), 192), :], gb[...], 1, 0).astype(BF16)
    for c in range(6):
        ga[pl.ds(3456 + 192 * c, 192), :] = r[:, 128 * c : 128 * c + 128]
    ga[pl.ds(4608 + S_ROWS, 512 - S_ROWS), :] = jnp.zeros((512 - S_ROWS, 128), BF16)
    tail = Reduce("a", net, at, ga, oa_ref, a1, ap1, a2, ob_ref)
    tail.start(0)

    net.got("g1x")
    g1_own_sum = g1_sum[...] + g1_far[...]
    put_small(S_G1, g1_own_sum[0:1, :])
    put_small(S_H1, g1_own_sum[8:9, :])
    ga[pl.ds(4608, S_ROWS), :] = small[...].astype(BF16)
    tail.start(1)
    big.second(1)
    big.second(0)
    tail.second(0)
    tail.second(1)
    big.own(1)
    big.own(0)
    tail.own(0)
    tail.own(1)
    net.put("gn1x", gn1_mine, gn1_far, at.xa)
    big.spread(1)
    big.spread(0)
    tail.spread(0)
    tail.spread(1)
    big.relay(1)
    big.relay(0)
    tail.relay(0)
    tail.relay(1)
    net.got("gn1x")

    @pl.loop(0, 4)
    def _(b):
        rows = pl.ds(up16(64 * b), 64)
        full = pl.ds(up16(256 * j + 64 * b), 64)
        g = gn1_mine[rows, :].astype(F32) + gn1_far[rows, :].astype(F32)
        n = n1[full, :]
        e = g * vec[V_G1 : V_G1 + 1, :]
        m = jnp.mean(e, axis=-1, keepdims=True)
        mn = jnp.mean(e * n, axis=-1, keepdims=True)
        ig_ref[rows, :] = gh1[full, :] + (e - m - n * mn) * scale1[full, 0:1]

    for reduce in (big, tail):
        reduce.end(1)
        reduce.end(0)
    tail.mirrored()
    net.finish()


def layer_call(*args):
    V = pltpu.VMEM
    sds = jax.ShapeDtypeStruct
    scratch = [
        V((512, 768), BF16), V((512, 768), BF16), V((512, 768), BF16), V((512, 768), F32), V((512, 128), F32),
        V((576, 768), BF16), V((576, 512), BF16), V((768, 512), BF16), V((3, 512, 512), F32), V((768, 768), BF16),
        V((384, 1536), BF16), V((384, 1536), BF16),
        V((512, 768), F32), V((512, 768), F32), V((512, 128), F32), V((512, 768), BF16), V((384, 512), BF16),
        V((384, 512), BF16), V((512, 1536), BF16), V((512, 1536), BF16), V((512, 768), BF16), V((512, 768), BF16),
        V((256, 384), F32), V((256, 384), F32), V((512, 768), F32), V((512, 768), BF16), V((32, 1536), F32),
        V((S_ROWS, 128), F32), V((192, 512), BF16), V((576, 512), BF16),
        V((16, 768), F32), V((16, 768), F32), V((16, 768), F32), V((16, 768), F32),
        V((512, 768), F32), V((256, 768), BF16), V((256, 768), BF16), V((256, 768), BF16), V((256, 768), BF16),
        V((9216, 128), BF16), V((5120, 128), BF16),
        V((2, 3, 1152, 128), BF16), V((2, 1152, 128), BF16), V((2, 7, 144, 128), BF16),
        V((2, 3, 640, 128), BF16), V((2, 640, 128), BF16), V((2, 7, 80, 128), BF16),
        V((8, 768), F32), V((1, 1536), F32), V((384, 1536), BF16), V((384, 1536), BF16),
        pltpu.SemaphoreType.DMA((160,)), pltpu.SemaphoreType.DMA((160,)), pltpu.SemaphoreType.DMA((8,)),
    ]
    vm = pl.BlockSpec(memory_space=V)
    return pl.pallas_call(
        layer_kernel,
        out_shape=(sds((256, 384), BF16), sds((256, 768), F32), sds((9216, 128), BF16), sds((5120, 128), BF16),
                   sds((5120, 128), BF16)),
        in_specs=[pl.BlockSpec(memory_space=pltpu.SMEM)] + [pl.BlockSpec(memory_space=pltpu.HBM)] * 6 + [vm] * 8,
        out_specs=(vm,) * 5,
        scratch_shapes=scratch,
        compiler_params=pltpu.CompilerParams(collective_id=0, has_side_effects=True, vmem_limit_bytes=60 << 20),
        name="layer",
    )(*args)


def finish_kernel(lo_in, ig_in, om_in, oa_in, ob_in, lo_out, ig_out, qkv_out, qvb_out, ow_out, out_bias, gain1, shift1, gain2, shift2,
                  up_out, up_bias, down_out, down_bias, qkv, ow, up, down, om, oa, ob, lo, ig,
                  sems, in_sems):
    j = lax.axis_index("grid")
    copies = []
    halves = [pl.ds(4608 * s, 4608) for s in range(2)]
    fetch = [
        pltpu.make_async_copy(src, dst, in_sems.at[n])
        for n, (src, dst) in enumerate(
            [(om_in.at[h], om.at[h]) for h in halves] + [(oa_in, oa), (ob_in, ob), (lo_in, lo), (ig_in, ig)])
    ]
    for copy in fetch:
        copy.start()

    def send(src, dst):
        copy = pltpu.make_async_copy(src, dst, sems.at[len(copies)])
        copy.start()
        copies.append(copy)

    for s, scr, dst in ((0, up, up_out), (1, down, down_out)):
        fetch[s].wait()
        for c in range(12):
            scr[:, 128 * c : 128 * c + 128] = om[4608 * s + 384 * c : 4608 * s + 384 * c + 384, :].astype(F32)
        send(scr, dst)
    fetch[2].wait()
    fetch[3].wait()
    for src, side in ((oa, j), (ob, 1 - j)):
        rows = pl.ds(pl.multiple_of(192 * side, 192), 192)
        for c in range(6):
            ow[rows, 128 * c : 128 * c + 128] = src[3456 + 192 * c : 3648 + 192 * c, :].astype(F32)
    send(ow, ow_out)
    fetch[4].wait()
    fetch[5].wait()
    send(lo, lo_out)
    send(ig, ig_out)
    for n in range(3):
        for src, side in ((oa, j), (ob, 1 - j)):
            rows = pl.ds(pl.multiple_of(192 * side, 192), 192)
            for c in range(6):
                at = 576 * c + 192 * n
                qkv[n, rows, 128 * c : 128 * c + 128] = src[at : at + 192, :].astype(F32)
        send(qkv.at[n], qkv_out.at[n])
    mine, other = (a[4608 : 4608 + S_ROWS, :].astype(F32) for a in (oa, ob))
    first, second = jnp.where(j == 0, mine, other), jnp.where(j == 0, other, mine)
    for n in range(2):
        qvb_out[n : n + 1, :] = jnp.concatenate(
            [part[2 * n + c : 2 * n + c + 1, : 128 - 64 * c] for part in (first, second) for c in range(2)], axis=1)
    for dst, row, count in ((out_bias, S_OB, 6), (gain1, S_G1, 6), (shift1, S_H1, 6), (gain2, S_G2, 6),
                            (shift2, S_H2, 6), (up_bias, S_UB, 12), (down_bias, S_DB, 3)):
        for c in range(count):
            dst[128 * c : 128 * c + 128] = mine[row + c]
    for copy in copies:
        copy.wait()


def finish(*args):
    V, hbm = pl.BlockSpec(memory_space=pltpu.VMEM), pl.BlockSpec(memory_space=pltpu.HBM)
    f = lambda *shape: jax.ShapeDtypeStruct(shape, F32)
    return pl.pallas_call(
        finish_kernel,
        out_shape=(jax.ShapeDtypeStruct((256, 384), BF16), f(256, 768), f(3, 384, 768), f(2, 384), f(384, 768),
                   f(768), f(768), f(768), f(768), f(768), f(384, 1536), f(1536), f(384, 1536), f(384)),
        in_specs=[hbm] * 5,
        out_specs=(hbm, hbm, hbm, V, hbm, V, V, V, V, V, hbm, V, hbm, V),
        scratch_shapes=[pltpu.VMEM((3, 384, 768), F32), pltpu.VMEM((384, 768), F32), pltpu.VMEM((384, 1536), F32),
                        pltpu.VMEM((384, 1536), F32), pltpu.VMEM((9216, 128), BF16), pltpu.VMEM((5120, 128), BF16),
                        pltpu.VMEM((5120, 128), BF16), pltpu.VMEM((256, 384), BF16), pltpu.VMEM((256, 768), F32),
                        pltpu.SemaphoreType.DMA((8,)), pltpu.SemaphoreType.DMA((6,))],
        compiler_params=pltpu.CompilerParams(vmem_limit_bytes=60 << 20),
        name="finish",
    )(*args)


def per_device(tokens, seq_lengths, cotangent, qkv_weight, qv_bias, out_weight, out_bias,
               first_gain, first_shift, second_gain, second_shift, up_weight, up_bias, down_weight, down_bias):
    return finish(*layer_call(
        seq_lengths, tokens, cotangent, qkv_weight, out_weight, up_weight, down_weight, qv_bias, out_bias,
        first_gain, first_shift, second_gain, second_shift, up_bias, down_bias))


def solution(mesh):
    placed = (
        P(("dp", "grid"), None), P("dp"), P(("dp", "grid"), None), P(None, "mp", None), P(None, "mp"),
        P("mp", None), P(), P(), P(), P(), P(), P("mp", "grid"), P("grid"), P("mp", "grid"), P("mp"),
    )
    return jax.shard_map(
        per_device,
        mesh=mesh,
        in_specs=placed,
        out_specs=(
            P(("dp", "grid"), "mp"), P(("dp", "grid"), None), P(None, "mp", None), P(None, "mp"), P("mp", None),
            P(), P(), P(), P(), P(), P("mp", "grid"), P("grid"), P("mp", "grid"), P("mp"),
        ),
        check_vma=False,
    )
```

```python
import functools

import jax
import jax.numpy as jnp
from jax import lax
from jax.experimental import pallas as pl
from jax.experimental.pallas import tpu as pltpu
from jax.sharding import PartitionSpec as P

HD = 64
EPS = 1e-05
NEG = -1e30
MESH = pl.DeviceIdType.MESH
F32, BF16 = jnp.float32, jnp.bfloat16


def dot(left, right, left_dim, right_dim):
    return lax.dot_general(
        left, right, (((left_dim,), (right_dim,)), ((), ())), preferred_element_type=F32
    )


def up16(value):
    return pl.multiple_of(value, 16)


def cols128(start, size):
    return pl.ds(pl.multiple_of(start, 128), size)


class Place:
    def __init__(self):
        dp = lax.axis_index("dp")
        self.i, self.j = lax.axis_index("mp"), lax.axis_index("grid")
        self.xh, self.y, self.z = lax.rem(dp, 2), lax.rem(lax.div(dp, 2), 4), lax.div(dp, 8)
        self.sib = {"grid": 1 - self.j}
        self.xa = {"mp": 1 - self.i}
        self.xb = {"dp": dp + 1 - 2 * self.xh, "mp": 1 - self.i}
        steps = (
            [2 * (lax.rem(self.y + d, 4) - self.y) for d in range(4)],
            [8 * (lax.rem(self.z + d, 4) - self.z) for d in range(4)],
        )
        flip = [0, 1 - 2 * self.xh]
        self.far = {"dp": dp + flip[1]}
        self.ring = [[{"dp": dp + r[d]} for d in (1, 2, 3)] for r in steps]
        self.eight = [[{"dp": dp + r[k // 2] + flip[k % 2]} for k in range(8)] for r in steps]

    def all(self):
        return [self.sib, self.xa, self.xb] + self.eight[0][1:] + self.eight[1][2:]


class Copies:
    def __init__(self, send, recv):
        self.send, self.recv, self.made = send, recv, {}

    def put(self, name, src, dst, device):
        at = len(self.made)
        copy = pltpu.make_async_remote_copy(
            src_ref=src, dst_ref=dst, send_sem=self.send.at[at], recv_sem=self.recv.at[at],
            device_id=device, device_id_type=MESH)
        copy.start()
        self.made[name] = copy

    def got(self, name):
        self.made[name].wait_recv()

    def finish(self):
        for copy in self.made.values():
            copy.wait_send()


class Reduce:
    def __init__(self, tag, net, at, src, out, r1, p1, r2, twin=None):
        self.tag, self.net, self.at, self.twin = tag, net, at, twin
        self.src, self.out, self.r1, self.p1, self.r2 = src, out, r1, p1, r2
        self.half = src.shape[0] // 2
        self.big, self.small = self.half // 4, self.half // 32
        self.pos = ((at.y, at.z), (at.z, at.y))
        self.rings = ((at.ring[0],), (at.ring[1],))
        self.eights = (at.eight[1], at.eight[0])

    def start(self, s):
        for d in (1, 2, 3):
            to = lax.rem(self.pos[s][0] + d, 4)
            self.net.put((self.tag, 1, s, d), self.src.at[pl.ds(up16(s * self.half + to * self.big), self.big)],
                         self.r1.at[s, d - 1], self.rings[s][0][d - 1])

    def part(self, s, k):
        across = self.at.xh + (k % 2) * (1 - 2 * self.at.xh)
        return (2 * lax.rem(self.pos[s][1] + k // 2, 4) + across) * self.small

    def second(self, s):
        base = s * self.half + self.pos[s][0] * self.big
        for d in (1, 2, 3):
            self.net.got((self.tag, 1, s, d))
        for k in (1, 2, 3, 4, 5, 6, 7, 0):
            off = self.part(s, k)
            rows = pl.ds(up16(off), self.small)
            total = self.src[pl.ds(up16(base + off), self.small), :].astype(F32)
            for e in range(3):
                total = total + self.r1[s, e, rows, :].astype(F32)
            self.p1[s, rows, :] = total.astype(BF16)
            if k:
                self.net.put((self.tag, 2, s, k), self.p1.at[s, rows], self.r2.at[s, k - 1], self.eights[s][k])

    def place(self, s):
        return pl.ds(up16(s * self.half + self.pos[s][0] * self.big + self.part(s, 0)), self.small)

    def own(self, s):
        for k in range(1, 8):
            self.net.got((self.tag, 2, s, k))
        total = self.p1[s, pl.ds(up16(self.part(s, 0)), self.small), :].astype(F32)
        for e in range(7):
            total = total + self.r2[s, e].astype(F32)
        rows = self.place(s)
        self.out[rows, :] = total.astype(BF16)
        for k in range(1, 8):
            self.net.put((self.tag, 3, s, k), self.out.at[rows], self.out.at[rows], self.eights[s][k])

    def piece(self, s, d, start, size):
        to = lax.rem(self.pos[s][0] + d, 4)
        return pl.ds(up16(s * self.half + to * self.big + start), size)

    def give(self, name, rows, device):
        self.net.put((self.tag,) + name, self.out.at[rows], self.out.at[rows], device)

    def mirror(self, s, d):
        if self.twin is not None:
            rows = self.piece(s, d, 0, self.big)
            self.net.put((self.tag, 6, s, d), self.out.at[rows], self.twin.at[rows], self.at.sib)

    def spread(self, s):
        for k in range(1, 8):
            self.net.got((self.tag, 3, s, k))
        for d in (1, 3):
            self.give((4, s, d), self.piece(s, 0, 0, self.big), self.rings[s][0][d - 1])
        self.mirror(s, 0)

    def relay(self, s):
        h = self.big // 2
        for d, start in ((1, 0), (3, h)):
            self.net.got((self.tag, 4, s, d))
            self.give((5, s, d), self.piece(s, 4 - d, start, h), self.rings[s][0][d - 1])
        for d in (1, 3):
            self.mirror(s, d)

    def end(self, s):
        for d in (1, 3):
            self.net.got((self.tag, 5, s, d))
        self.mirror(s, 2)

    def mirrored(self):
        for s in (0, 1):
            for d in range(4):
                self.net.got((self.tag, 6, s, d))


class Narrow(Reduce):
    def __init__(self, tag, net, at, src, out, r1, p1, r2, p2, rx):
        super().__init__(tag, net, at, src, out, r1, p1, r2)
        self.p2, self.rx, self.small = p2, rx, self.half // 16
        self.seconds = (at.ring[1], at.ring[0])

    def second(self, s):
        base = s * self.half + self.pos[s][0] * self.big
        for d in (1, 2, 3):
            self.net.got((self.tag, 1, s, d))
        for d in (1, 2, 3, 0):
            off = lax.rem(self.pos[s][1] + d, 4) * self.small
            rows = pl.ds(up16(off), self.small)
            total = self.src[pl.ds(up16(base + off), self.small), :].astype(F32)
            for e in range(3):
                total = total + self.r1[s, e, rows, :].astype(F32)
            self.p1[s, rows, :] = total.astype(BF16)
            if d:
                self.net.put((self.tag, 2, s, d), self.p1.at[s, rows], self.r2.at[s, d - 1], self.seconds[s][d - 1])

    def third(self):
        for s in (0, 1):
            for d in (1, 2, 3):
                self.net.got((self.tag, 2, s, d))
            total = self.p1[s, pl.ds(up16(self.pos[s][1] * self.small), self.small), :].astype(F32)
            for e in range(3):
                total = total + self.r2[s, e].astype(F32)
            self.p2[s] = total.astype(BF16)
        self.net.put((self.tag, 7), self.p2.at[1 - self.at.xh], self.rx, self.at.far)

    def start_of(self, s):
        return s * self.half + self.pos[s][0] * self.big + self.pos[s][1] * self.small

    def middle(self):
        self.net.got((self.tag, 7))
        where = self.start_of(0) + self.at.xh * (self.start_of(1) - self.start_of(0))
        rows = pl.ds(up16(where), self.small)
        self.out[rows, :] = (self.p2[self.at.xh].astype(F32) + self.rx[...].astype(F32)).astype(BF16)
        self.give((8,), rows, self.at.far)

    def back(self):
        self.net.got((self.tag, 8))
        for s in (0, 1):
            rows = pl.ds(up16(self.start_of(s)), self.small)
            for d in (1, 2, 3):
                self.give((3, s, d), rows, self.seconds[s][d - 1])

    def spread(self, s):
        for d in (1, 2, 3):
            self.net.got((self.tag, 3, s, d))
        for d in (1, 3):
            self.give((4, s, d), self.piece(s, 0, 0, self.big), self.rings[s][0][d - 1])


def column_sum8(values):
    return jnp.sum(values.reshape(values.shape[0] // 8, 8, values.shape[1]), axis=0)


S_QB, S_VB, S_OB, S_G1, S_H1, S_G2, S_H2, S_UB, S_DB, S_ROWS = 0, 2, 4, 10, 16, 22, 28, 34, 46, 64
V_OB, V_G1, V_H1, V_G2, V_H2, V_UB, V_DB = range(7)


def layer_kernel(
    length_ref, tokens, cotangent, qkv_in, out_in, up_in, down_in, qvb_in, ob_in, g1_in, h1_in, g2_in, h2_in,
    ub_in, db_in,
    lo_ref, ig_ref, om_ref, oa_ref, ob_ref,
    x_all, cot, normed1, n1, scale1, wown, qkvt, attt, probs, out_all, up_oth, down_oth,
    h1, n2, scale2, normed2, n2t, cott, hid, gpre, gn, gn_sib, mo, mo_sib, gh1, gb, acc, small, gattt, gt,
    g1_own, g1_sib, g1_sum, g1_far, gn1_keep, gn1_out, gn1_in, gn1_mine, gn1_far,
    gm, ga, m1, mp1, m2, mp2, mx, a1, ap1, a2, vec, vec_up, up_ref, down_ref, send, recv, near,
):
    at = Place()
    i, j = at.i, at.j
    mine, theirs = pl.ds(up16(256 * j), 256), pl.ds(up16(256 * (1 - j)), 256)
    ihalf = pl.ds(up16(384 * i), 384)
    local = [(tokens, x_all.at[mine])]
    local += [(qkv_in.at[t, pl.ds(up16(192 * j), 192)], wown.at[pl.ds(192 * t, 192)]) for t in range(3)]
    local += [(cotangent, cot.at[mine]), (out_in, out_all.at[ihalf]), (up_in, up_ref), (down_in, down_ref)]
    local = [pltpu.make_async_copy(src, dst, near.at[n]) for n, (src, dst) in enumerate(local)]
    for copy in local:
        copy.start()
    bar = pltpu.get_barrier_semaphore()
    peers = at.all()
    for peer in peers:
        pl.semaphore_signal(bar, inc=1, device_id=peer, device_id_type=MESH)
    pl.semaphore_wait(bar, len(peers))
    net = Copies(send, recv)
    ipart, opart = cols128(384 * i, 384), cols128(384 * (1 - i), 384)

    net.put("tok", tokens, x_all.at[mine], at.sib)
    net.put("cot", cotangent, cot.at[mine], at.sib)
    odd_y, odd_z = lax.rem(at.y, 2), lax.rem(at.z, 2)
    quarter = 2 * odd_y + odd_z
    across = (quarter + 2 - 4 * odd_y, quarter + 1 - 2 * odd_z)
    weights = (("up", up_in, up_oth), ("down", down_in, down_oth))

    def weight_rows(q, start, size):
        return pl.ds(up16(96 * q + start), size)

    for name, src, dst in weights:
        for n, peer in enumerate((at.xa, at.xb)):
            rows = weight_rows(quarter, 48 * n, 48)
            net.put((name, "x", n), src.at[rows], dst.at[rows], peer)
    for n, peer in enumerate((at.xa, at.xb)):
        part = 192 * j + 96 * n
        net.put(("out", n), out_in.at[pl.ds(up16(part), 96)], out_all.at[pl.ds(up16(384 * i + part), 96)], peer)

    def pass_on(which):
        name, _, dst = weights[which]
        for n in range(2):
            net.got((name, "x", n))
        for axis in range(2):
            for n in range(2):
                rows = weight_rows(quarter, 48 * n, 48)
                net.put((name, axis, n), dst.at[rows], dst.at[rows], at.ring[axis][2 * n])

    def pass_further(which):
        name, _, dst = weights[which]
        for axis in range(2):
            net.got((name, 1 - axis, axis))
            for n in range(2):
                rows = weight_rows(across[1 - axis], 48 * axis + 32 * n, 32 - 16 * n)
                net.put((name, "d", axis, n), dst.at[rows], dst.at[rows], at.ring[axis][2 * n])

    def weight_here(which):
        name = weights[which][0]
        for axis in range(2):
            net.got((name, axis, axis))
            for n in range(2):
                net.got((name, "d", axis, n))

    def first_norm(start):
        @pl.loop(0, 4)
        def _(b):
            rows = pl.ds(up16(start + 64 * b), 64)
            v = x_all[rows, :].astype(F32)
            c = v - jnp.mean(v, axis=-1, keepdims=True)
            sc = lax.rsqrt(jnp.mean(c * c, axis=-1, keepdims=True) + EPS)
            n = c * sc
            n1[rows, :] = n
            scale1[rows, :] = jnp.broadcast_to(sc, (64, 128))
            normed1[rows, :] = (n * vec[V_G1 : V_G1 + 1, :] + vec[V_H1 : V_H1 + 1, :]).astype(BF16)

    for n, ref in enumerate((ob_in, g1_in, h1_in, g2_in, h2_in)):
        vec[n : n + 1, :] = ref[...].reshape(1, 768)
    vec[V_DB : V_DB + 1, 0:384] = db_in[...].reshape(1, 384)
    vec_up[...] = ub_in[...].reshape(1, 1536)
    local[0].wait()
    first_norm(256 * j)
    net.got("tok")
    first_norm(256 * (1 - j))
    for copy in local[1:4]:
        copy.wait()

    ones = jnp.ones((16, 512), BF16)
    line = lax.broadcasted_iota(jnp.int32, (16, 192), 0)

    def bias_columns(n):
        b = jnp.where(j == 0, qvb_in[n : n + 1, 0:192], qvb_in[n : n + 1, 192:384])
        t1 = b.astype(BF16).astype(F32)
        t2 = (b - t1).astype(BF16).astype(F32)
        terms = jnp.where(line == 0, t1, jnp.where(line == 1, t2, jnp.where(line == 2, b - t1 - t2, 0.0)))
        return dot(terms.astype(BF16), ones, 0, 0)

    for t in range(3):
        r = dot(wown[192 * t : 192 * t + 192, :], normed1[...], 1, 1)
        if t == 0:
            r = (r + bias_columns(0)).astype(BF16).astype(F32) * (HD**-0.5)
        if t == 2:
            r = r + bias_columns(1)
        qkvt[192 * t : 192 * t + 192, :] = r.astype(BF16)

    pass_on(0)
    length = length_ref[0]
    own_rows = 384 * i + 192 * j
    for h in range(3):
        for qb in range(2):
            kr = 256 * (qb + 1)
            qc = slice(256 * qb, 256 * qb + 256)
            kt = qkvt[192 + 64 * h : 256 + 64 * h, 0:kr]
            s = dot(kt, qkvt[64 * h : 64 * h + 64, qc], 0, 0)
            kp = lax.broadcasted_iota(jnp.int32, (kr, 256), 0)
            qp = lax.broadcasted_iota(jnp.int32, (kr, 256), 1) + 256 * qb
            s = jnp.where((kp == qp) | ((kp < qp) & (qp < length)), s, NEG)
            e = jnp.exp(s - jnp.max(s, axis=0, keepdims=True))
            p = e * (1.0 / jnp.sum(e, axis=0, keepdims=True))
            probs[h, 0:kr, qc] = p
            o = dot(qkvt[384 + 64 * h : 448 + 64 * h, 0:kr], p.astype(BF16), 1, 0)
            attt[pl.ds(up16(own_rows + 64 * h), 64), qc] = o.astype(BF16)
        rows = pl.ds(up16(own_rows + 64 * h), 64)
        for n, peer in enumerate((at.xa, at.sib)):
            net.put(("att", h, n), attt.at[rows], attt.at[rows], peer)

    pass_on(1)

    for copy in local[4:]:
        copy.wait()
    net.got("cot")
    cott[...] = cot[:, ipart].T
    small[...] = jnp.zeros_like(small)

    def put_small(row, value):
        for c in range(value.shape[1] // 128):
            small[row + c : row + c + 1, :] = value[:, 128 * c : 128 * c + 128]

    put_small(S_DB, jnp.sum(cot[:, ipart].astype(F32), axis=0, keepdims=True))
    far_rows = 384 * (1 - i) + 192 * j
    pass_further(0)
    for n in range(2):
        net.got(("out", n))
    rows = pl.ds(up16(far_rows), 192)
    net.put("outs", out_all.at[rows], out_all.at[rows], at.sib)
    pass_further(1)
    for h in range(3):
        net.got(("att", h, 0))
        rows = pl.ds(up16(far_rows + 64 * h), 64)
        net.put(("att", h, 2), attt.at[rows], attt.at[rows], at.sib)
    net.got("outs")
    for h in range(3):
        for n in (1, 2):
            net.got(("att", h, n))

    @pl.loop(0, 4)
    def _(b):
        rows = pl.ds(up16(128 * b), 128)
        v = x_all[rows, :].astype(F32) + dot(attt[:, cols128(128 * b, 128)], out_all[...], 0, 0)
        v = v + vec[V_OB : V_OB + 1, :]
        h1[rows, :] = v
        c = v - jnp.mean(v, axis=-1, keepdims=True)
        sc = lax.rsqrt(jnp.mean(c * c, axis=-1, keepdims=True) + EPS)
        n = c * sc
        n2[rows, :] = n
        scale2[rows, :] = jnp.broadcast_to(sc, (128, 128))
        normed2[rows, :] = (n * vec[V_G2 : V_G2 + 1, :] + vec[V_H2 : V_H2 + 1, :]).astype(BF16)

    n2t[...] = normed2[:, ipart].T
    weight_here(0)
    weight_here(1)

    @pl.loop(0, 6)
    def _(c):
        cs = cols128(256 * c, 256)
        pre = dot(normed2[:, ipart], up_ref[:, cs], 1, 0) + dot(normed2[:, opart], up_oth[:, cs], 1, 0)
        pre = pre + vec_up[:, cs]
        g = dot(cot[:, ipart], down_ref[:, cs], 1, 0) + dot(cot[:, opart], down_oth[:, cs], 1, 0)
        k = 0.7978845608028654
        sq = pre * pre
        t = jnp.tanh(pre * (k + (k * 0.044715) * sq))
        half = 0.5 + 0.5 * t
        hid[:, cs] = (pre * half).astype(BF16)
        slope = half + (pre * half) * (1.0 - t) * (k + (3 * 0.044715 * k) * sq)
        gp = (g * slope).astype(BF16)
        gpre[:, cs] = gp
        ub = jnp.sum(gp.astype(F32), axis=0, keepdims=True)
        acc[24:25, cs] = ub

    for c in range(2):
        rows = pl.ds(256 * c, 256)
        gn[rows, ipart] = dot(gpre[rows, :], up_ref[...], 1, 1).astype(BF16)
        gn[rows, opart] = dot(gpre[rows, :], up_oth[...], 1, 1).astype(BF16)
        net.put(("gn", c), gn.at[rows], gn_sib.at[rows], at.sib)

    big = Narrow("m", net, at, gm, om_ref, m1, mp1, m2, mp2, mx)
    for s, left, right in ((1, cott, hid), (0, n2t, gpre)):
        @pl.loop(0, 6)
        def _(c):
            r = dot(left[...], right[:, cols128(256 * c, 256)], 1, 0).astype(BF16)
            for b in range(2):
                gm[pl.ds(up16(4608 * s + 384 * (2 * c + b)), 384), :] = r[:, 128 * b : 128 * b + 128]
        big.start(s)

    mo[...] = dot(hid[theirs, :], down_ref[...], 1, 1)
    net.put("mo", mo, mo_sib, at.sib)
    lo_part = dot(hid[mine, :], down_ref[...], 1, 1) + h1[mine, ipart] + vec[V_DB : V_DB + 1, 0:384]

    acc[0:24, 0:768] = jnp.zeros((24, 768), F32)
    for c in range(2):
        net.got(("gn", c))

    @pl.loop(0, 8)
    def _(b):
        rows = pl.ds(up16(64 * b), 64)
        g = gn[rows, :].astype(F32) + gn_sib[rows, :].astype(F32)
        n = n2[rows, :]
        e = g * vec[V_G2 : V_G2 + 1, :]
        m = jnp.mean(e, axis=-1, keepdims=True)
        mn = jnp.mean(e * n, axis=-1, keepdims=True)
        v = cot[rows, :].astype(F32) + (e - m - n * mn) * scale2[rows, 0:1]
        gh1[rows, :] = v
        low = v.astype(BF16)
        gb[rows, :] = low
        acc[0:8, 0:768] += column_sum8(g * n)
        acc[8:16, 0:768] += column_sum8(g)
        acc[16:24, 0:768] += column_sum8(low.astype(F32))

    put_small(S_G2, jnp.sum(acc[0:8, 0:768], axis=0, keepdims=True))
    put_small(S_H2, jnp.sum(acc[8:16, 0:768], axis=0, keepdims=True))
    put_small(S_OB, jnp.sum(acc[16:24, 0:768], axis=0, keepdims=True))
    put_small(S_UB, acc[24:25, :])

    gattt[...] = dot(out_all[pl.ds(up16(own_rows), 192), :], gb[...], 1, 1).astype(BF16)
    net.got("mo")
    lo_ref[...] = (lo_part + mo_sib[...]).astype(BF16)

    for h in range(3):
        hs = slice(64 * h, 64 * h + 64)
        gk, gv = [], []
        for qb in range(2):
            kr = 256 * (qb + 1)
            qc = slice(256 * qb, 256 * qb + 256)
            p = probs[h, 0:kr, qc]
            gat = gattt[hs, qc]
            g = dot(qkvt[384 + 64 * h : 448 + 64 * h, 0:kr], gat, 0, 0)
            delta = jnp.sum(p * g, axis=0, keepdims=True)
            gs = (p * (g - delta)).astype(BF16)
            gt[hs, qc] = (dot(qkvt[192 + 64 * h : 256 + 64 * h, 0:kr], gs, 1, 0) * (HD**-0.5)).astype(BF16)
            gk.append(dot(qkvt[hs, qc], gs, 1, 1))
            gv.append(dot(gat, p.astype(BF16), 1, 1))
        for base, parts in ((192, gk), (384, gv)):
            rows = slice(base + 64 * h, base + 64 * h + 64)
            gt[rows, 0:256] = (parts[0] + parts[1][:, 0:256]).astype(BF16)
            gt[rows, 256:512] = parts[1][:, 256:512].astype(BF16)

    @pl.loop(0, 2)
    def _(b):
        rows = pl.ds(up16(128 * b), 128)
        r = dot(gt[:, cols128(256 * (1 - j) + 128 * b, 128)], wown[...], 0, 0)
        gn1_out[rows, :] = r.astype(BF16)
        gn1_keep[pl.ds(up16(256 * (1 - j) + 128 * b), 128), :] = r

    net.put("gn1", gn1_out, gn1_in, at.sib)

    @pl.loop(0, 2)
    def _(b):
        r = dot(gt[:, cols128(256 * j + 128 * b, 128)], wown[...], 0, 0)
        gn1_keep[pl.ds(up16(256 * j + 128 * b), 128), :] = r

    acc[0:16, 0:768] = jnp.zeros((16, 768), F32)

    @pl.loop(0, 8)
    def _(b):
        rows = pl.ds(up16(64 * b), 64)
        g = gn1_keep[rows, :]
        acc[0:8, 0:768] += column_sum8(g * n1[rows, :])
        acc[8:16, 0:768] += column_sum8(g)

    for n in range(2):
        g1_own[8 * n : 8 * n + 8, :] = jnp.broadcast_to(
            jnp.sum(acc[8 * n : 8 * n + 8, 0:768], axis=0, keepdims=True), (8, 768))
    net.put("g1", g1_own, g1_sib, at.sib)
    for base, row in ((0, S_QB), (384, S_VB)):
        r = dot(ones, gt[base : base + 192, :], 1, 1)
        small[row : row + 1, :] = r[0:1, 0:128]
        small[row + 1 : row + 2, 0:64] = r[0:1, 128:192]
    net.got("g1")
    g1_sum[...] = g1_own[...] + g1_sib[...]
    net.put("g1x", g1_sum, g1_far, at.xa)
    net.got("gn1")
    half_sum = gn1_keep[mine, :] + gn1_in[...].astype(F32)
    gn1_mine[...] = half_sum.astype(BF16)
    for n in range(3):
        r = dot(gt[192 * n : 192 * n + 192, :], normed1[...], 1, 0).astype(BF16)
        for c in range(6):
            ga[pl.ds(576 * c + 192 * n, 192), :] = r[:, 128 * c : 128 * c + 128]
    r = dot(attt[pl.ds(up16(own_rows), 192), :], gb[...], 1, 0).astype(BF16)
    for c in range(6):
        ga[pl.ds(3456 + 192 * c, 192), :] = r[:, 128 * c : 128 * c + 128]
    ga[pl.ds(4608 + S_ROWS, 512 - S_ROWS), :] = jnp.zeros((512 - S_ROWS, 128), BF16)
    tail = Reduce("a", net, at, ga, oa_ref, a1, ap1, a2, ob_ref)
    tail.start(0)

    net.got("g1x")
    g1_own_sum = g1_sum[...] + g1_far[...]
    put_small(S_G1, g1_own_sum[0:1, :])
    put_small(S_H1, g1_own_sum[8:9, :])
    ga[pl.ds(4608, S_ROWS), :] = small[...].astype(BF16)
    tail.start(1)
    big.second(1)
    big.second(0)
    tail.second(0)
    tail.second(1)
    big.third()
    tail.own(0)
    tail.own(1)
    big.middle()
    big.back()
    net.put("gn1x", gn1_mine, gn1_far, at.xa)
    tail.spread(0)
    tail.spread(1)
    big.spread(1)
    big.spread(0)
    tail.relay(0)
    tail.relay(1)
    big.relay(1)
    big.relay(0)
    net.got("gn1x")

    @pl.loop(0, 4)
    def _(b):
        rows = pl.ds(up16(64 * b), 64)
        full = pl.ds(up16(256 * j + 64 * b), 64)
        g = gn1_mine[rows, :].astype(F32) + gn1_far[rows, :].astype(F32)
        n = n1[full, :]
        e = g * vec[V_G1 : V_G1 + 1, :]
        m = jnp.mean(e, axis=-1, keepdims=True)
        mn = jnp.mean(e * n, axis=-1, keepdims=True)
        ig_ref[rows, :] = gh1[full, :] + (e - m - n * mn) * scale1[full, 0:1]

    for reduce in (tail, big):
        reduce.end(1)
        reduce.end(0)
    tail.mirrored()
    net.finish()


def layer_call(*args):
    V = pltpu.VMEM
    sds = jax.ShapeDtypeStruct
    scratch = [
        V((512, 768), BF16), V((512, 768), BF16), V((512, 768), BF16), V((512, 768), F32), V((512, 128), F32),
        V((576, 768), BF16), V((576, 512), BF16), V((768, 512), BF16), V((3, 512, 512), F32), V((768, 768), BF16),
        V((384, 1536), BF16), V((384, 1536), BF16),
        V((512, 768), F32), V((512, 768), F32), V((512, 128), F32), V((512, 768), BF16), V((384, 512), BF16),
        V((384, 512), BF16), V((512, 1536), BF16), V((512, 1536), BF16), V((512, 768), BF16), V((512, 768), BF16),
        V((256, 384), F32), V((256, 384), F32), V((512, 768), F32), V((512, 768), BF16), V((32, 1536), F32),
        V((S_ROWS, 128), F32), V((192, 512), BF16), V((576, 512), BF16),
        V((16, 768), F32), V((16, 768), F32), V((16, 768), F32), V((16, 768), F32),
        V((512, 768), F32), V((256, 768), BF16), V((256, 768), BF16), V((256, 768), BF16), V((256, 768), BF16),
        V((9216, 128), BF16), V((5120, 128), BF16),
        V((2, 3, 1152, 128), BF16), V((2, 1152, 128), BF16), V((2, 3, 288, 128), BF16),
        V((2, 288, 128), BF16), V((288, 128), BF16),
        V((2, 3, 640, 128), BF16), V((2, 640, 128), BF16), V((2, 7, 80, 128), BF16),
        V((8, 768), F32), V((1, 1536), F32), V((384, 1536), BF16), V((384, 1536), BF16),
        pltpu.SemaphoreType.DMA((160,)), pltpu.SemaphoreType.DMA((160,)), pltpu.SemaphoreType.DMA((8,)),
    ]
    vm = pl.BlockSpec(memory_space=V)
    return pl.pallas_call(
        layer_kernel,
        out_shape=(sds((256, 384), BF16), sds((256, 768), F32), sds((9216, 128), BF16), sds((5120, 128), BF16),
                   sds((5120, 128), BF16)),
        in_specs=[pl.BlockSpec(memory_space=pltpu.SMEM)] + [pl.BlockSpec(memory_space=pltpu.HBM)] * 6 + [vm] * 8,
        out_specs=(vm,) * 5,
        scratch_shapes=scratch,
        compiler_params=pltpu.CompilerParams(collective_id=0, has_side_effects=True, vmem_limit_bytes=60 << 20),
        name="layer",
    )(*args)


def finish_kernel(lo_in, ig_in, om_in, oa_in, ob_in, lo_out, ig_out, qkv_out, qvb_out, ow_out, out_bias, gain1, shift1, gain2, shift2,
                  up_out, up_bias, down_out, down_bias, qkv, ow, up, down, om, oa, ob, lo, ig,
                  sems, in_sems):
    j = lax.axis_index("grid")
    copies = []
    halves = [pl.ds(4608 * s, 4608) for s in range(2)]
    fetch = [
        pltpu.make_async_copy(src, dst, in_sems.at[n])
        for n, (src, dst) in enumerate(
            [(om_in.at[h], om.at[h]) for h in halves] + [(oa_in, oa), (ob_in, ob), (lo_in, lo), (ig_in, ig)])
    ]
    for copy in fetch:
        copy.start()

    def send(src, dst):
        copy = pltpu.make_async_copy(src, dst, sems.at[len(copies)])
        copy.start()
        copies.append(copy)

    for s, scr, dst in ((0, up, up_out), (1, down, down_out)):
        fetch[s].wait()
        for c in range(12):
            scr[:, 128 * c : 128 * c + 128] = om[4608 * s + 384 * c : 4608 * s + 384 * c + 384, :].astype(F32)
        send(scr, dst)
    fetch[2].wait()
    fetch[3].wait()
    for src, side in ((oa, j), (ob, 1 - j)):
        rows = pl.ds(pl.multiple_of(192 * side, 192), 192)
        for c in range(6):
            ow[rows, 128 * c : 128 * c + 128] = src[3456 + 192 * c : 3648 + 192 * c, :].astype(F32)
    send(ow, ow_out)
    fetch[4].wait()
    fetch[5].wait()
    send(lo, lo_out)
    send(ig, ig_out)
    for n in range(3):
        for src, side in ((oa, j), (ob, 1 - j)):
            rows = pl.ds(pl.multiple_of(192 * side, 192), 192)
            for c in range(6):
                at = 576 * c + 192 * n
                qkv[n, rows, 128 * c : 128 * c + 128] = src[at : at + 192, :].astype(F32)
        send(qkv.at[n], qkv_out.at[n])
    mine, other = (a[4608 : 4608 + S_ROWS, :].astype(F32) for a in (oa, ob))
    first, second = jnp.where(j == 0, mine, other), jnp.where(j == 0, other, mine)
    for n in range(2):
        qvb_out[n : n + 1, :] = jnp.concatenate(
            [part[2 * n + c : 2 * n + c + 1, : 128 - 64 * c] for part in (first, second) for c in range(2)], axis=1)
    for dst, row, count in ((out_bias, S_OB, 6), (gain1, S_G1, 6), (shift1, S_H1, 6), (gain2, S_G2, 6),
                            (shift2, S_H2, 6), (up_bias, S_UB, 12), (down_bias, S_DB, 3)):
        for c in range(count):
            dst[128 * c : 128 * c + 128] = mine[row + c]
    for copy in copies:
        copy.wait()


def finish(*args):
    V, hbm = pl.BlockSpec(memory_space=pltpu.VMEM), pl.BlockSpec(memory_space=pltpu.HBM)
    f = lambda *shape: jax.ShapeDtypeStruct(shape, F32)
    return pl.pallas_call(
        finish_kernel,
        out_shape=(jax.ShapeDtypeStruct((256, 384), BF16), f(256, 768), f(3, 384, 768), f(2, 384), f(384, 768),
                   f(768), f(768), f(768), f(768), f(768), f(384, 1536), f(1536), f(384, 1536), f(384)),
        in_specs=[hbm] * 5,
        out_specs=(hbm, hbm, hbm, V, hbm, V, V, V, V, V, hbm, V, hbm, V),
        scratch_shapes=[pltpu.VMEM((3, 384, 768), F32), pltpu.VMEM((384, 768), F32), pltpu.VMEM((384, 1536), F32),
                        pltpu.VMEM((384, 1536), F32), pltpu.VMEM((9216, 128), BF16), pltpu.VMEM((5120, 128), BF16),
                        pltpu.VMEM((5120, 128), BF16), pltpu.VMEM((256, 384), BF16), pltpu.VMEM((256, 768), F32),
                        pltpu.SemaphoreType.DMA((8,)), pltpu.SemaphoreType.DMA((6,))],
        compiler_params=pltpu.CompilerParams(vmem_limit_bytes=60 << 20),
        name="finish",
    )(*args)


def per_device(tokens, seq_lengths, cotangent, qkv_weight, qv_bias, out_weight, out_bias,
               first_gain, first_shift, second_gain, second_shift, up_weight, up_bias, down_weight, down_bias):
    return finish(*layer_call(
        seq_lengths, tokens, cotangent, qkv_weight, out_weight, up_weight, down_weight, qv_bias, out_bias,
        first_gain, first_shift, second_gain, second_shift, up_bias, down_bias))


def solution(mesh):
    placed = (
        P(("dp", "grid"), None), P("dp"), P(("dp", "grid"), None), P(None, "mp", None), P(None, "mp"),
        P("mp", None), P(), P(), P(), P(), P(), P("mp", "grid"), P("grid"), P("mp", "grid"), P("mp"),
    )
    return jax.shard_map(
        per_device,
        mesh=mesh,
        in_specs=placed,
        out_specs=(
            P(("dp", "grid"), "mp"), P(("dp", "grid"), None), P(None, "mp", None), P(None, "mp"), P("mp", None),
            P(), P(), P(), P(), P(), P("mp", "grid"), P("grid"), P("mp", "grid"), P("mp"),
        ),
        check_vma=False,
    )
```
